512 devices in a mesh: stream: 16 (over z_lo, y), cross: 32 (over z_hi, x, core).
Axes of the slice: x: 4, y: 4, z: 16 (z_hi: 4, z_lo: 4; z = z_hi * 4 + z_lo), core: 2. Of those that a mesh axis runs over, the one named last changes fastest.
Arguments:
- vof: bfloat16 [6144, 512], P(('stream', 'cross')), may hold values from 0 to 1
- target: bfloat16 [6144, 512], P(('stream', 'cross')), may hold values from -21 to 21
- neighbours: int32 [6144, 26], P(('stream', 'cross')), may hold values from -1 to 6143, as said below
- live_blocks: int32 [512], P(('stream', 'cross')), may hold values from 2 to 12, as said below
- pick: int32 [512, 2], P(('stream', 'cross')), may hold values from -1 to 191, as said below
- w_first: bfloat16 [125, 128], replicated, may hold values from -0.5 to 0.5
- w_mid: bfloat16 [2, 128, 128], replicated, may hold values from -0.5 to 0.5
- w_last: bfloat16 [128], replicated, may hold values from -0.5 to 0.5
Outputs:
- prediction: float32 [4096, 512], P(('stream', 'cross'))
- grad_first: float32 [125, 128], replicated
- grad_mid: float32 [2, 128, 128], replicated
- grad_last: float32 [128], replicated
The draws below stay inside these ranges and needn't reach their ends.
Inputs may be any that keep to these rules, and one draw needn't show every extreme that they name: Home slots 0 to live_blocks[d] - 1 of device d hold interface blocks and the rest are empty; in every slab 8 devices hold more than 6 blocks and the others at most 6. `neighbours`: an entry names a live home slot of a device whose stream index and cross index each differ from those of the block's own device by at most one. `pick`: in each slab every live home slot 6 + j of the device with cross index c is named, as c * 6 + j, by exactly one entry of one device of that slab; devices holding more than 6 blocks name none.
All inputs are finite; a program needn't handle non-finite values.
Results may differ from the reference program's by a relative error of at most 0.003.
The reference program's roundings to bfloat16 on the way count: a program that leaves them out, or rounds other values in their place, can miss the bound.
Values may be sent and summed in bfloat16 or wider, within the bound.
A program may use at most 128 MiB of HBM per device.

```python
import jax
import jax.numpy as jnp
from jax import lax

FEAT = 125
HID = 128
BE = 8
KEEP = 6
BLK_DEV = 12
RECV = 2
TRAIN = 8
CELLS = 512
SLABS = 16
SLAB_DEVS = 32
QUOTA = 8
NDEV = 512
NBLK = 6144
NTRAIN = 4096


def load_plan(key):
    order_key, extra_key, low_key = jax.random.split(jax.random.fold_in(key, 7), 3)
    orders = jax.vmap(lambda inner: jax.random.permutation(inner, SLAB_DEVS))(jax.random.split(order_key, SLABS))
    ranking = jnp.argsort(orders, axis=1, stable=True).astype(jnp.int32)
    ranking = ((ranking - ranking[:, -1:]) % SLAB_DEVS).astype(jnp.int32)
    busy_mask = ranking < QUOTA
    surplus = jax.random.randint(extra_key, (SLABS, SLAB_DEVS), (KEEP + 1) // 2, KEEP + 1)
    surplus = jnp.where(ranking == 0, KEEP, surplus)
    smaller = jax.random.randint(low_key, (SLABS, SLAB_DEVS), 2, KEEP + 1)
    holding = jnp.where(busy_mask, KEEP + surplus, smaller).astype(jnp.int32)
    surplus = jnp.where(busy_mask, surplus, 0).astype(jnp.int32)
    return (ranking, surplus, holding)


def draw_live_blocks(key, part):
    ranking, surplus, holding = load_plan(key)
    return holding.reshape(NDEV)


def draw_pick(key, part):
    ranking, surplus, holding = load_plan(key)
    pool = jnp.arange(SLAB_DEVS * KEEP).astype(jnp.int32)
    owner = pool // KEEP
    within = pool % KEEP
    used = within[None, :] < surplus[:, owner]
    number = jnp.cumsum(used.astype(jnp.int32), axis=1) - 1
    place = (ranking - QUOTA)[:, :, None] * RECV + jnp.arange(RECV).astype(jnp.int32)[None, None, :]
    hit = used[:, None, None, :] & (number[:, None, None, :] == place[:, :, :, None])
    chosen = jnp.sum(jnp.where(hit, pool + 1, 0), axis=-1) - 1
    return chosen.reshape(NDEV, RECV).astype(jnp.int32)


def draw_neighbours(key, part):
    ranking, surplus, holding = load_plan(key)
    key = jax.random.fold_in(key, 9)
    step_key, column_key, slot_key, gap_key = jax.random.split(key, 4)
    live_flat = holding.reshape(-1)
    blocks = jnp.arange(NBLK).astype(jnp.int32)
    home_device = blocks // BLK_DEV
    slab_of = home_device // SLAB_DEVS
    column_of = home_device % SLAB_DEVS
    stepping = jax.random.randint(step_key, (NBLK, 26), -1, 2)
    other = slab_of[:, None] + stepping
    inside = (other >= 0) & (other < SLABS)
    column = jnp.clip(column_of[:, None] + jax.random.randint(column_key, (NBLK, 26), -1, 2), 0, SLAB_DEVS - 1)
    device = jnp.clip(other, 0, SLABS - 1) * SLAB_DEVS + column
    within = jax.random.randint(slot_key, (NBLK, 26), 0, live_flat[device])
    absent = jax.random.randint(gap_key, (NBLK, 26), 0, 4) == 0
    result = jnp.where(inside & jnp.logical_not(absent), device * BLK_DEV + within, -1).astype(jnp.int32)
    return result.at[NBLK - 2, 0].set(NBLK - 1).astype(jnp.int32)


def draw_target(key, part):
    key = jax.random.fold_in(key, 11)
    rising = 1.0 + 2.0 * jnp.arange(NBLK, dtype=jnp.float32)[:, None] / max(NBLK - 1, 1)
    values = 0.5 + jnp.clip(jax.random.normal(key, (NBLK, CELLS), jnp.float32), -6.0, 6.0)
    return (rising * values).astype(jnp.bfloat16)


def level_of(own_key, shape, shards, low, largest):
    factor_of = 1.0
    for dim, blocks in shards:
        heights = jax.random.uniform(jax.random.fold_in(jax.random.fold_in(own_key, 6), dim), (blocks,), jnp.float32, low / len(shards), largest / len(shards))
        factor_of = factor_of * jnp.repeat(jnp.exp(heights), shape[dim] // blocks).reshape((-1,) + (1,) * (len(shape) - 1 - dim))
    return factor_of


def noise(stream_key, shape, scale, reach, kind=jnp.bfloat16):
    values = jax.random.normal(stream_key, shape, jnp.float32) * scale
    return jnp.minimum(jnp.maximum(values, -reach), reach).astype(kind)


def setup_inputs(seed: int = 0) -> dict:
    splits = jax.random.split(jax.random.key(seed), 9)
    return {
        "vof": jnp.clip(1.0 * jax.random.uniform(splits[0], (NBLK, CELLS), jnp.float32) ** level_of(splits[0], (NBLK, CELLS), ((0, 512),), -0.2, 0.2), 0.0, 1.0).astype(jnp.bfloat16),
        "target": draw_target(jax.random.fold_in(splits[8], 71), 0),
        "neighbours": draw_neighbours(jax.random.fold_in(splits[8], 71), 0),
        "live_blocks": draw_live_blocks(jax.random.fold_in(splits[8], 71), 0),
        "pick": draw_pick(jax.random.fold_in(splits[8], 71), 0),
        "w_first": noise(splits[5], (FEAT, HID), FEAT ** -0.5, 0.5),
        "w_mid": noise(splits[6], (2, HID, HID), HID ** -0.5, 0.5),
        "w_last": noise(splits[7], (HID,), HID ** -0.5, 0.5),
    }


def assemble(center, border, block_edge):
    number = center.shape[0]
    pieces = jnp.concatenate([border[:, :13], center[:, None], border[:, 13:]], axis=1)
    shaped = pieces.reshape(number, 3, 3, 3, block_edge, block_edge, block_edge)
    shaped = shaped.transpose(0, 1, 4, 2, 5, 3, 6).reshape(number, 3 * block_edge, 3 * block_edge, 3 * block_edge)
    lower = block_edge - 2
    upper = 2 * block_edge + 2
    return shaped[:, lower:upper, lower:upper, lower:upper]


def stencil(padded, block_edge):
    columns = []
    for along_x in range(5):
        for along_y in range(5):
            for along_z in range(5):
                window = padded[:, along_x:along_x + block_edge, along_y:along_y + block_edge, along_z:along_z + block_edge]
                columns.append(window.reshape(-1))
    return jnp.stack(columns)


def contract_rows(former, latter):
    return lax.dot_general(former, latter, (((0,), (0,)), ((), ())), preferred_element_type=jnp.float32)


def contract_cols(former, latter):
    return lax.dot_general(former, latter, (((1,), (1,)), ((), ())), preferred_element_type=jnp.float32)


def train_terms(features, target_row, weight_mask, w_first, w_mid, w_last, loss_scale):
    hidden_one = jnp.tanh(contract_rows(w_first, features)).astype(jnp.bfloat16)
    hidden_two = jnp.tanh(contract_rows(w_mid[0], hidden_one)).astype(jnp.bfloat16)
    hidden_three = jnp.tanh(contract_rows(w_mid[1], hidden_two)).astype(jnp.bfloat16)
    predicted = jnp.dot(w_last, hidden_three, preferred_element_type=jnp.float32) * weight_mask
    residual = ((predicted - target_row.astype(jnp.float32)) * weight_mask / loss_scale).astype(jnp.bfloat16)
    grad_last = jnp.dot(hidden_three, residual, preferred_element_type=jnp.float32)
    slope_three = 1.0 - jnp.square(hidden_three.astype(jnp.float32))
    delta_three = (w_last.astype(jnp.float32)[:, None] * residual.astype(jnp.float32)[None, :] * slope_three).astype(jnp.bfloat16)
    grad_third = contract_cols(hidden_two, delta_three)
    slope_two = 1.0 - jnp.square(hidden_two.astype(jnp.float32))
    delta_two = (jnp.dot(w_mid[1], delta_three, preferred_element_type=jnp.float32) * slope_two).astype(jnp.bfloat16)
    grad_second = contract_cols(hidden_one, delta_two)
    slope_one = 1.0 - jnp.square(hidden_one.astype(jnp.float32))
    delta_one = (jnp.dot(w_mid[0], delta_two, preferred_element_type=jnp.float32) * slope_one).astype(jnp.bfloat16)
    grad_first = contract_cols(features, delta_one)
    return predicted, grad_first, jnp.stack([grad_second, grad_third]), grad_last


def reference(vof, target, neighbours, live_blocks, pick, w_first, w_mid, w_last):
    device_total = SLABS * SLAB_DEVS
    padded_table = jnp.concatenate([vof, jnp.zeros((1, CELLS), vof.dtype)], axis=0)
    lookup = jnp.where(neighbours < 0, NBLK, neighbours).astype(jnp.int32)
    loss_scale = float(CELLS * KEEP * device_total)
    keep_range = jnp.arange(KEEP).astype(jnp.int32)

    def one_device(totals, device):
        slab_index = device // SLAB_DEVS
        chosen = pick[device]
        safe_pick = jnp.maximum(chosen, 0)
        source = (slab_index * SLAB_DEVS + safe_pick // KEEP) * BLK_DEV + KEEP + safe_pick % KEEP
        blocks = jnp.concatenate([device * BLK_DEV + keep_range, source.astype(jnp.int32)])
        padded = assemble(vof[blocks], padded_table[lookup[blocks]], BE)
        block_mask = jnp.concatenate([keep_range < live_blocks[device], chosen >= 0]).astype(jnp.float32)
        weight_mask = jnp.repeat(block_mask, CELLS)
        predicted, grad_first, grad_mid, grad_last = train_terms(stencil(padded, BE), target[blocks].reshape(-1), weight_mask, w_first, w_mid, w_last, loss_scale)
        totals = (totals[0] + grad_first, totals[1] + grad_mid, totals[2] + grad_last)
        return totals, predicted.reshape(TRAIN, CELLS)

    initial = (jnp.zeros((FEAT, HID), jnp.float32), jnp.zeros((2, HID, HID), jnp.float32), jnp.zeros((HID,), jnp.float32))
    totals, predicted = lax.scan(one_device, initial, jnp.arange(device_total).astype(jnp.int32))
    return predicted.reshape(NTRAIN, CELLS), totals[0], totals[1], totals[2]
```

```python
import jax
import jax.numpy as jnp
from jax import lax
from jax.experimental import pallas as pl
from jax.experimental.pallas import tpu as pltpu
from jax.sharding import PartitionSpec as P

MESH = pl.DeviceIdType.MESH
F32 = jnp.float32
BF16 = jnp.bfloat16

KEEP = 6
HOME = 12
ROWS = 768
WIN = 384
SCALE = 1572864.0
SLABS = 16
CROSS = 32
PIECE = 12
PLANE = 32
VMEM = pl.BlockSpec(memory_space=pltpu.VMEM)
SMEM = pl.BlockSpec(memory_space=pltpu.SMEM)


def lanes(shape):
    return lax.broadcasted_iota(jnp.int32, shape, len(shape) - 1)


def shift(x, by):
    by = by % 128
    return x if by == 0 else pltpu.roll(x, by, x.ndim - 1)


def spread(rows, store, stride, first):
    lane = lanes(rows[:, :128].shape)
    for y in range(8):
        total = jnp.zeros_like(rows[:, :128])
        for x in range(8):
            source = rows[:, 128 * (x // 2) : 128 * (x // 2) + 128]
            moved = shift(source, stride * x + first - (64 * (x % 2) + 8 * y))
            low = stride * x + first
            total = jnp.where((lane >= low) & (lane < low + 8), moved, total)
        store(y, total)


def remote(src, dst, send, recv, device):
    return pltpu.make_async_remote_copy(
        src_ref=src,
        dst_ref=dst,
        send_sem=send,
        recv_sem=recv,
        device_id=device,
        device_id_type=MESH,
    )


STEPS = [(a, b) for a in (-1, 0, 1) for b in (-1, 0, 1) if (a, b) != (0, 0)]


def halo_kernel(vof_ref, nbr_ref, table_ref, lookup_ref, own, send_sem, recv_sem):
    slab = lax.axis_index("stream")
    cross = lax.axis_index("cross")
    partner = [
        (lax.rem(slab + a + SLABS, SLABS), lax.rem(cross + b + CROSS, CROSS)) for a, b in STEPS
    ]
    barrier = pltpu.get_barrier_semaphore()
    for device in partner:
        pl.semaphore_signal(barrier, inc=1, device_id=device, device_id_type=MESH)

    def keep(y, tile):
        own[pl.ds(y, HOME, stride=8), :] = tile

    spread(vof_ref[...].astype(F32), keep, 12, 2)
    table_ref[4] = own[...].astype(BF16)

    pl.semaphore_wait(barrier, len(STEPS))
    copies = []
    for k, (a, b) in enumerate(STEPS):
        copy = remote(
            table_ref.at[4],
            table_ref.at[(1 - a) * 3 + 1 - b],
            send_sem.at[k],
            recv_sem.at[len(STEPS) - 1 - k],
            partner[k],
        )
        copy.start()
        copies.append(copy)

    nbr = nbr_ref[...]
    device = (nbr * 43691) >> 19
    slot = nbr - 12 * device
    place = (((device >> 5) - slab + 1) * 3 + ((device & 31) - cross + 1)) * HOME + slot
    lookup_ref[...] = jnp.where(nbr < 0, 9 * HOME, place)

    for copy in copies:
        copy.wait_send()
    for k, (a, b) in enumerate(STEPS):
        remote(
            table_ref.at[4],
            table_ref.at[(1 + a) * 3 + 1 + b],
            send_sem.at[k],
            recv_sem.at[k],
            partner[k],
        ).wait_recv()


def dot_t(a, b):
    return lax.dot_general(a, b, (((0,), (0,)), ((), ())), preferred_element_type=F32)


def dot_n(a, b):
    return lax.dot_general(a, b, (((1,), (1,)), ((), ())), preferred_element_type=F32)


def dot(a, b):
    return jnp.dot(a, b, preferred_element_type=F32)


def build_first(w1_ref, w1p, t):
    w1p[...] = jnp.zeros_like(w1p)
    w1p[0:125, :] = w1_ref[...].astype(F32)
    w1 = w1p[...].astype(BF16)
    k = lax.broadcasted_iota(jnp.int32, (WIN, 128), 0)
    f = lanes((WIN, 128))
    m = k & 63
    ax = (m * 43) >> 9
    zp = m - 12 * ax
    ay = k >> 6
    code = jnp.where((m < 60) & (ay < 5), 25 * ax + 5 * ay + zp, -1000)
    for z in range(8):
        hit = (f == code - z) & (zp >= z) & (zp < z + 5)
        select = jnp.where(hit, 1.0, 0.0).astype(BF16)
        t[:, 128 * z : 128 * z + 128] = dot(select, w1).astype(BF16)


def build_window(b, lookup_ref, tab, pad, xs):
    lane = lanes((8, 128))
    zp = lane - 12 * ((lane * 43) >> 9)
    for dy in range(3):
        row = []
        for dx in range(3):
            got = []
            for dz in range(3):
                k = 9 * dx + 3 * dy + dz
                if k == 13:
                    at = 4 * HOME + b
                else:
                    at = lookup_ref[b, k if k < 13 else k - 1]
                got.append(tab[pl.ds(pl.multiple_of(at * 8, 8), 8), :])
            row.append(
                jnp.where(zp < 2, shift(got[0], -8), jnp.where(zp < 10, got[1], shift(got[2], 8)))
            )
        low = jnp.where(lane < 24, shift(row[0], -72), shift(row[1], 24))
        high = jnp.where(lane < 72, shift(row[1], -24), shift(row[2], 72))
        pad[0, 8 * dy : 8 * dy + 8, :] = low
        pad[1, 8 * dy : 8 * dy + 8, :] = high
    for half in range(2):
        a = [pad[half, 6 + ay : 14 + ay, :] for ay in range(5)]
        odd = [shift(a[1], 64), shift(a[3], 64)]
        made = []
        for x in range(4):
            inside = (lane >= 12 * x) & (lane < 12 * x + 64)
            made.append(
                [
                    shift(jnp.where(inside, a[0], odd[0]), -12 * x),
                    shift(jnp.where(inside, a[2], odd[1]), -12 * x),
                    shift(a[4], -12 * x),
                ]
            )
        for pair in range(2):
            for g in range(3):
                both = jnp.concatenate([made[2 * pair][g], made[2 * pair + 1][g]], axis=0)
                base = pl.multiple_of(64 * b, 64) + 32 * half + 16 * pair
                xs[pl.ds(pl.multiple_of(base, 16), 16), 128 * g : 128 * g + 128] = both.astype(BF16)


CHUNK = 256


def local_kernel(
    lookup_ref,
    live_ref,
    table_ref,
    target_ref,
    w1_ref,
    wmid_ref,
    wlast_ref,
    grad_ref,
    extra_ref,
    home_ref,
    tab,
    tt,
    pad,
    xs,
    w1p,
    t,
    bd2,
    bd3,
    wle,
    h1,
    h2,
    h3,
    d1,
    d2,
    d3,
    r2,
    pt,
    flat,
    sums,
):
    for i in range(9):
        tab[96 * i : 96 * i + 96, :] = table_ref[i].astype(F32)
    tab[864:872, :] = jnp.zeros((8, 128), F32)

    def keep(y, tile):
        tt[pl.ds(y, HOME, stride=8), :] = tile

    spread(target_ref[...].astype(F32), keep, 8, 0)
    build_first(w1_ref, w1p, t)
    for ref, i in ((bd2, 0), (bd3, 1)):
        ref[...] = jnp.zeros_like(ref)
        ref[0:128, 0:128] = wmid_ref[i]
        ref[128:256, 128:256] = wmid_ref[i]
    wl = wlast_ref[...].astype(F32)
    sub = lax.broadcasted_iota(jnp.int32, (128, 128), 0)
    for z in range(8):
        wle[:, 128 * z : 128 * z + 128] = jnp.where((sub & 7) == z, wl, 0.0).astype(BF16)

    @pl.loop(0, HOME)
    def _(b):
        build_window(b, lookup_ref, tab, pad, xs)

    live = live_ref[0]
    lane = lanes((8, 128))

    @pl.loop(0, ROWS // CHUNK)
    def _(c):
        at = pl.ds(pl.multiple_of(c * CHUNK, CHUNK), CHUNK)
        x = xs[at, :]
        predicted = jnp.zeros((CHUNK, 128), F32)
        for j in range(4):
            col = slice(256 * j, 256 * j + 256)
            a = jnp.tanh(dot(x, t[:, col])).astype(BF16)
            h1[at, col] = a
            a = jnp.tanh(dot(a, bd2[...])).astype(BF16)
            h2[at, col] = a
            a = jnp.tanh(dot(a, bd3[...])).astype(BF16)
            h3[at, col] = a
            predicted += dot_n(a, wle[:, col])
        for i in range(CHUNK // 64):
            b = c * (CHUNK // 64) + i
            tile = jnp.zeros((8, 128), F32)
            for k in range(8):
                part = predicted[64 * i + 8 * k : 64 * i + 8 * k + 8]
                tile = jnp.where(((lane >> 3) & 7) == k, part, tile)
            rows = pl.ds(pl.multiple_of(b * 8, 8), 8)
            mask = jnp.where(b < live, 1.0, 0.0).astype(F32)
            pt[rows, :] = tile
            res = ((tile * mask - tt[rows, :]) * mask / SCALE).astype(BF16).astype(F32)
            for k in range(4):
                both = jnp.concatenate(
                    [
                        jnp.where((lane >> 3) == 2 * k, res, 0.0),
                        jnp.where((lane >> 3) == 2 * k + 1, res, 0.0),
                    ],
                    axis=0,
                )
                r2[pl.ds(pl.multiple_of(b * 64 + 16 * k, 16), 16), :] = both.astype(BF16)
        rr = r2[at, :]
        for j in range(4):
            col = slice(256 * j, 256 * j + 256)
            h = h3[at, col].astype(F32)
            d = (dot(rr, wle[:, col]) * (1.0 - h * h)).astype(BF16)
            d3[at, col] = d
            h = h2[at, col].astype(F32)
            d = (dot_n(d, bd3[...]) * (1.0 - h * h)).astype(BF16)
            d2[at, col] = d
            h = h1[at, col].astype(F32)
            d = (dot_n(d, bd2[...]) * (1.0 - h * h)).astype(BF16)
            d1[at, col] = d

    for b in range(KEEP):
        mask = jnp.where(b < live, 1.0, 0.0).astype(F32)
        home_ref[8 * b : 8 * b + 8, :] = pt[8 * b : 8 * b + 8, :] * mask
    for i in range(3):
        at = 8 * (KEEP + 2 * i)
        extra_ref[i] = jnp.where(lane < 64, pt[at : at + 8, :], pt[at + 8 : at + 16, :])

    second = jnp.zeros((128, 128), F32)
    third = jnp.zeros((128, 128), F32)
    for z in range(8):
        col = slice(128 * z, 128 * z + 128)
        second += dot_t(h1[:, col], d2[:, col])
        third += dot_t(h2[:, col], d3[:, col])
    flat[0:128, :] = second
    flat[128:256, :] = third
    total = jnp.zeros((WIN, 128), F32)
    xv = xs[...]
    for j in range(4):
        g = dot_t(xv, d1[:, 256 * j : 256 * j + 256])
        for i in range(2):
            z = 2 * j + i
            part = g[:, 128 * i : 128 * i + 128]
            total += part if z == 0 else pltpu.roll(part, WIN - z, 0)
    sums[...] = total
    for ax in range(5):
        for ay in range(5):
            at = 64 * ay + 12 * ax
            to = 256 + 25 * ax + 5 * ay
            flat[to : to + 5, :] = sums[at : at + 5, :]
    last = jnp.zeros((1, 128), F32)
    for j in range(4):
        g = dot_t(r2[...], h3[:, 256 * j : 256 * j + 256])
        for i in range(2):
            z = 2 * j + i
            part = jnp.where((sub & 7) == z, g[:, 128 * i : 128 * i + 128], 0.0)
            last += jnp.sum(part, axis=0, keepdims=True)
    flat[381:382, :] = last
    flat[382:384, :] = jnp.zeros((2, 128), F32)
    for i in range(PLANE):
        grad_ref[i] = flat[PIECE * i : PIECE * i + PIECE, :]


def sum_kernel(
    pick_ref,
    grad_ref,
    extra_ref,
    home_ref,
    pred_ref,
    gfirst_ref,
    gmid_ref,
    glast_ref,
    rs,
    lo,
    hi,
    ag,
    eb,
    pk,
    ob,
    rb,
    pt,
    flat,
    rs_s,
    rs_r,
    ag_s,
    ag_r,
    lo_s,
    lo_r,
    hi_s,
    hi_r,
    eb_s,
    eb_r,
    pk_s,
    pk_r,
    ob_s,
    ob_r,
):
    slab = lax.axis_index("stream")
    cross = lax.axis_index("cross")
    zlo, y = slab // 4, lax.rem(slab, 4)
    zhi, xc = cross // 8, lax.rem(cross, 8)
    me = y * 8 + xc

    def of_plane(p):
        return (zlo * 4 + p // 8, zhi * 8 + lax.rem(p, 8))

    def of_lo(q):
        return (q * 4 + y, cross)

    def of_hi(q):
        return (slab, q * 8 + xc)

    def of_row(q):
        return (slab, zhi * 8 + q)

    def others(number, mine, body):
        def step(k, carry):
            body(k, lax.rem(mine + k, number))
            return carry

        lax.fori_loop(1, number, step, 0)

    barrier = pltpu.get_barrier_semaphore()

    def greet(place):
        def body(k, q):
            pl.semaphore_signal(barrier, inc=1, device_id=place(q), device_id_type=MESH)

        return body

    others(PLANE, me, greet(of_plane))
    others(4, zlo, greet(of_lo))
    others(4, zhi, greet(of_hi))

    lane = lanes((8, 128))
    pk[zhi] = jnp.where(lane < 64, pick_ref[0, 0], pick_ref[0, 1])
    rs[me] = grad_ref[me]
    eb[xc] = extra_ref[...]

    pl.semaphore_wait(barrier, PLANE - 1 + 3 + 3)

    def plane_copy(k, q, slot):
        return remote(grad_ref.at[q], rs.at[slot], rs_s.at[k], rs_r.at[slot], of_plane(q))

    def row_copy(k, q, slot):
        return remote(extra_ref, eb.at[slot], eb_s.at[k], eb_r.at[slot], of_row(q))

    def pick_copy(k, q, slot):
        return remote(pk.at[zhi], pk.at[slot], pk_s.at[k], pk_r.at[slot], of_hi(q))

    def lo_copy(k, q, slot):
        return remote(lo.at[zlo], lo.at[slot], lo_s.at[k], lo_r.at[slot], of_lo(q))

    def hi_copy(k, q, slot):
        return remote(hi.at[zhi], hi.at[slot], hi_s.at[k], hi_r.at[slot], of_hi(q))

    def out_copy(k, q, slot):
        return remote(ob.at[q], rb.at[slot], ob_s.at[k], ob_r.at[slot], of_hi(q))

    def all_copy(k, q, slot):
        return remote(ag.at[me], ag.at[slot], ag_s.at[k], ag_r.at[slot], of_plane(q))

    def start(number, mine, copy):
        others(number, mine, lambda k, q: copy(k, q, mine).start())

    def arrive(number, mine, copy):
        others(number, mine, lambda k, q: copy(k, q, q).wait_recv())

    def sent(number, mine, copy):
        others(number, mine, lambda k, q: copy(k, q, mine).wait_send())

    start(PLANE, me, plane_copy)
    start(4, zhi, pick_copy)
    start(8, xc, row_copy)

    arrive(PLANE, me, plane_copy)
    total = rs[0]
    for i in range(1, PLANE):
        total += rs[i]
    lo[zlo] = total
    start(4, zlo, lo_copy)

    arrive(4, zhi, pick_copy)
    arrive(8, xc, row_copy)
    outs = [jnp.zeros((8, 128), F32) for _ in range(4)]
    wants = [pk[q] for q in range(4)]
    for d in range(8):
        for i in range(3):
            tile = eb[d, i]
            swapped = shift(tile, 64)
            name = (zhi * 8 + d) * KEEP + 2 * i
            first = jnp.where(lane < 64, tile, swapped)
            other = jnp.where(lane < 64, swapped, tile)
            for q in range(4):
                outs[q] = jnp.where(wants[q] == name, first, outs[q])
                outs[q] = jnp.where(wants[q] == name + 1, other, outs[q])
    for q in range(4):
        ob[q] = outs[q]
    start(4, zhi, out_copy)
    rb[zhi] = ob[zhi]

    arrive(4, zlo, lo_copy)
    hi[zhi] = (lo[0] + lo[1]) + (lo[2] + lo[3])
    start(4, zhi, hi_copy)

    arrive(4, zhi, out_copy)
    tile = (rb[0] + rb[1]) + (rb[2] + rb[3])
    pt[0:48, :] = home_ref[...]
    pt[48:56, :] = tile
    pt[56:64, :] = shift(tile, 64)
    parts = [jnp.zeros((8, 128), F32) for _ in range(4)]
    for yy in range(8):
        v = pt[pl.ds(yy, 8, stride=8), :]
        for x in range(8):
            low = 64 * (x % 2) + 8 * yy
            inside = (lane >= low) & (lane < low + 8)
            parts[x // 2] = jnp.where(inside, shift(v, low - 8 * x), parts[x // 2])
    for i in range(4):
        pred_ref[:, 128 * i : 128 * i + 128] = parts[i]

    arrive(4, zhi, hi_copy)
    ag[me] = (hi[0] + hi[1]) + (hi[2] + hi[3])
    start(PLANE, me, all_copy)
    sent(PLANE, me, plane_copy)
    sent(8, xc, row_copy)
    sent(4, zhi, pick_copy)
    sent(4, zlo, lo_copy)
    sent(4, zhi, out_copy)
    sent(4, zhi, hi_copy)
    arrive(PLANE, me, all_copy)
    for i in range(PLANE):
        flat[PIECE * i : PIECE * i + PIECE, :] = ag[i]
    gmid_ref[0] = flat[0:128, :]
    gmid_ref[1] = flat[128:256, :]
    gfirst_ref[...] = flat[256:381, :]
    glast_ref[...] = flat[381:382, :]
    sent(PLANE, me, all_copy)


def dma(n):
    return pltpu.SemaphoreType.DMA((n,))


def halo(vof, neighbours):
    return pl.pallas_call(
        halo_kernel,
        out_shape=(
            jax.ShapeDtypeStruct((9, 96, 128), BF16),
            jax.ShapeDtypeStruct((HOME, 26), jnp.int32),
        ),
        in_specs=[VMEM, VMEM],
        out_specs=(VMEM, VMEM),
        scratch_shapes=[pltpu.VMEM((96, 128), F32), dma(8), dma(8)],
        compiler_params=pltpu.CompilerParams(
            collective_id=0, has_side_effects=True, vmem_limit_bytes=16 << 20
        ),
        name="halo",
    )(vof, neighbours)


def local_terms(lookup, live_blocks, table, target, w_first, w_mid, w_last):
    big = pltpu.VMEM((ROWS, 1024), BF16)
    return pl.pallas_call(
        local_kernel,
        out_shape=(
            jax.ShapeDtypeStruct((PLANE, PIECE, 128), F32),
            jax.ShapeDtypeStruct((3, 8, 128), F32),
            jax.ShapeDtypeStruct((48, 128), F32),
        ),
        in_specs=[SMEM, SMEM, VMEM, VMEM, VMEM, VMEM, VMEM],
        out_specs=(VMEM, VMEM, VMEM),
        scratch_shapes=[
            pltpu.VMEM((872, 128), F32),
            pltpu.VMEM((96, 128), F32),
            pltpu.VMEM((2, 24, 128), F32),
            pltpu.VMEM((ROWS, WIN), BF16),
            pltpu.VMEM((128, 128), F32),
            pltpu.VMEM((WIN, 1024), BF16),
            pltpu.VMEM((256, 256), BF16),
            pltpu.VMEM((256, 256), BF16),
            pltpu.VMEM((128, 1024), BF16),
            big,
            big,
            big,
            big,
            big,
            big,
            pltpu.VMEM((ROWS, 128), BF16),
            pltpu.VMEM((96, 128), F32),
            pltpu.VMEM((384, 128), F32),
            pltpu.VMEM((384, 128), F32),
        ],
        compiler_params=pltpu.CompilerParams(vmem_limit_bytes=40 << 20),
        name="local_terms",
    )(lookup, live_blocks, table, target, w_first, w_mid, w_last)


def sum_all(pick, grads, extra, home):
    piece = pltpu.VMEM((PLANE, PIECE, 128), F32)
    small = pltpu.VMEM((4, PIECE, 128), F32)
    return pl.pallas_call(
        sum_kernel,
        out_shape=(
            jax.ShapeDtypeStruct((8, 512), F32),
            jax.ShapeDtypeStruct((125, 128), F32),
            jax.ShapeDtypeStruct((2, 128, 128), F32),
            jax.ShapeDtypeStruct((1, 128), F32),
        ),
        in_specs=[SMEM, VMEM, VMEM, VMEM],
        out_specs=(VMEM, VMEM, VMEM, VMEM),
        scratch_shapes=[
            piece,
            small,
            small,
            piece,
            pltpu.VMEM((8, 3, 8, 128), F32),
            pltpu.VMEM((4, 8, 128), jnp.int32),
            pltpu.VMEM((4, 8, 128), F32),
            pltpu.VMEM((4, 8, 128), F32),
            pltpu.VMEM((64, 128), F32),
            pltpu.VMEM((384, 128), F32),
            dma(PLANE),
            dma(PLANE),
            dma(PLANE),
            dma(PLANE),
            dma(4),
            dma(4),
            dma(4),
            dma(4),
            dma(8),
            dma(8),
            dma(4),
            dma(4),
            dma(4),
            dma(4),
        ],
        compiler_params=pltpu.CompilerParams(
            collective_id=1, has_side_effects=True, vmem_limit_bytes=16 << 20
        ),
        name="sum_all",
    )(pick, grads, extra, home)


def shards(vof, target, neighbours, live_blocks, pick, w_first, w_mid, w_last):
    table, lookup = halo(vof, neighbours)
    grads, extra, home = local_terms(
        lookup, live_blocks, table, target, w_first, w_mid, w_last.reshape(1, 128)
    )
    pred, gfirst, gmid, glast = sum_all(pick, grads, extra, home)
    return pred, gfirst, gmid, glast.reshape(128)


def solution(mesh):
    both = ("stream", "cross")
    return jax.shard_map(
        shards,
        mesh=mesh,
        in_specs=(
            P(both, None),
            P(both, None),
            P(both, None),
            P(both),
            P(both, None),
            P(),
            P(),
            P(),
        ),
        out_specs=(P(both, None), P(), P(), P()),
        check_vma=False,
    )
```

```python
import jax
import jax.numpy as jnp
from jax import lax
from jax.experimental import pallas as pl
from jax.experimental.pallas import tpu as pltpu
from jax.sharding import PartitionSpec as P

MESH = pl.DeviceIdType.MESH
F32 = jnp.float32
BF16 = jnp.bfloat16

KEEP = 6
HOME = 12
ROWS = 768
WIN = 384
SCALE = 1572864.0
SLABS = 16
CROSS = 32
PIECE = 12
VMEM = pl.BlockSpec(memory_space=pltpu.VMEM)


def lanes(shape):
    return lax.broadcasted_iota(jnp.int32, shape, len(shape) - 1)


def shift(x, by):
    by = by % 128
    return x if by == 0 else pltpu.roll(x, by, x.ndim - 1)


def spread(parts, store, stride, first):
    lane = lanes(parts[0].shape)
    for y in range(8):
        total = jnp.zeros_like(parts[0])
        for x in range(8):
            moved = shift(parts[x // 2], stride * x + first - (64 * (x % 2) + 8 * y))
            low = stride * x + first
            total = jnp.where((lane >= low) & (lane < low + 8), moved, total)
        store(y, total)


def keep_in(ref):
    def store(y, tile):
        ref[pl.ds(y, HOME, stride=8), :] = tile

    return store


def remote(src, dst, send, recv, device):
    return pltpu.make_async_remote_copy(
        src_ref=src,
        dst_ref=dst,
        send_sem=send,
        recv_sem=recv,
        device_id=device,
        device_id_type=MESH,
    )


def dot_t(a, b):
    return lax.dot_general(a, b, (((0,), (0,)), ((), ())), preferred_element_type=F32)


def dot_n(a, b):
    return lax.dot_general(a, b, (((1,), (1,)), ((), ())), preferred_element_type=F32)


def dot(a, b):
    return jnp.dot(a, b, preferred_element_type=F32)


def build_first(w1_ref, w1p, t):
    w1p[...] = jnp.zeros_like(w1p)
    w1p[0:125, :] = w1_ref[...].astype(F32)
    w1 = w1p[...].astype(BF16)
    k = lax.broadcasted_iota(jnp.int32, (WIN, 128), 0)
    f = lanes((WIN, 128))
    m = k & 63
    ax = (m * 43) >> 9
    zp = m - 12 * ax
    ay = k >> 6
    code = jnp.where((m < 60) & (ay < 5), 25 * ax + 5 * ay + zp, -1000)
    for z in range(8):
        hit = (f == code - z) & (zp >= z) & (zp < z + 5)
        select = jnp.where(hit, 1.0, 0.0).astype(BF16)
        t[:, 128 * z : 128 * z + 128] = dot(select, w1).astype(BF16)


def build_window(b, lookup_ref, tab, pad, xs):
    lane = lanes((8, 128))
    zp = lane - 12 * ((lane * 43) >> 9)
    for dy in range(3):
        row = []
        for dx in range(3):
            got = []
            for dz in range(3):
                k = 9 * dx + 3 * dy + dz
                if k == 13:
                    at = 4 * HOME + b
                else:
                    at = lookup_ref[b, k if k < 13 else k - 1]
                got.append(tab[at])
            row.append(
                jnp.where(zp < 2, shift(got[0], -8), jnp.where(zp < 10, got[1], shift(got[2], 8)))
            )
        low = jnp.where(lane < 24, shift(row[0], -72), shift(row[1], 24))
        high = jnp.where(lane < 72, shift(row[1], -24), shift(row[2], 72))
        pad[0, 8 * dy : 8 * dy + 8, :] = low
        pad[1, 8 * dy : 8 * dy + 8, :] = high
    for half in range(2):
        a = [pad[half, 6 + ay : 14 + ay, :] for ay in range(5)]
        odd = [shift(a[1], 64), shift(a[3], 64)]
        made = []
        for x in range(4):
            inside = (lane >= 12 * x) & (lane < 12 * x + 64)
            made.append(
                [
                    shift(jnp.where(inside, a[0], odd[0]), -12 * x),
                    shift(jnp.where(inside, a[2], odd[1]), -12 * x),
                    shift(a[4], -12 * x),
                ]
            )
        for pair in range(2):
            for g in range(3):
                both = jnp.concatenate([made[2 * pair][g], made[2 * pair + 1][g]], axis=0)
                base = pl.multiple_of(64 * b, 64) + 32 * half + 16 * pair
                xs[pl.ds(pl.multiple_of(base, 16), 16), 128 * g : 128 * g + 128] = both.astype(BF16)


STEPS = [(a, b) for a in (-1, 0, 1) for b in (-1, 0, 1) if (a, b) != (0, 0)]
STEPS.sort(key=lambda step: (step[1] == 0, step[0] == 0))
CHUNK = 256


def train_kernel(
    vof_hbm,
    target_hbm,
    nbr_hbm,
    live_hbm,
    pick_hbm,
    w1_hbm,
    wmid_hbm,
    wlast_hbm,
    sum_ref,
    pred_ref,
    vof_ref,
    target_ref,
    nbr_ref,
    live_ref,
    pick_ref,
    w1_ref,
    wmid_ref,
    wlast_ref,
    lookup_vec,
    lookup_ref,
    packed,
    table,
    tall,
    tab,
    tt,
    pad,
    xs,
    w1p,
    t,
    bd2,
    bd3,
    wle,
    h1,
    h2,
    h3,
    d1,
    d2,
    d3,
    r2,
    pt,
    flat,
    sums,
    extra,
    eb,
    pk,
    ob,
    rb,
    cs,
    half,
    hs,
    rs,
    zb,
    in_s,
    halo_s,
    halo_r,
    eb_s,
    eb_r,
    pk_s,
    pk_r,
    ob_s,
    ob_r,
    cs_s,
    cs_r,
    rs_s,
    rs_r,
    zb_s,
    zb_r,
    ag_s,
    ag_r,
):
    fetches = [
        pltpu.make_async_copy(src, dst, in_s.at[i])
        for i, (src, dst) in enumerate(
            (
                (vof_hbm, vof_ref),
                (nbr_hbm, nbr_ref),
                (w1_hbm, w1_ref),
                (wmid_hbm, wmid_ref),
                (wlast_hbm, wlast_ref),
                (target_hbm, target_ref),
                (live_hbm, live_ref),
                (pick_hbm, pick_ref),
            )
        )
    ]
    for fetch in fetches:
        fetch.start()

    slab = lax.axis_index("stream")
    cross = lax.axis_index("cross")
    zlo, y = slab // 4, lax.rem(slab, 4)
    zhi, xc = cross // 8, lax.rem(cross, 8)
    x, core = xc // 2, lax.rem(xc, 2)
    zz = zhi * 4 + zlo
    xy = y * 4 + x
    pair = (slab, cross + 1 - 2 * core)

    def of_xy(q):
        return (zlo * 4 + q // 4, zhi * 8 + 2 * lax.rem(q, 4) + core)

    def of_z(q):
        return (lax.rem(q, 4) * 4 + y, (q // 4) * 8 + xc)

    def of_hi(q):
        return (slab, q * 8 + xc)

    def of_row(q):
        return (slab, zhi * 8 + q)

    def others(number, mine, body):
        def step(k, carry):
            body(k, lax.rem(mine + k, number))
            return carry

        lax.fori_loop(1, number, step, 0)

    table[...] = jnp.zeros_like(table)

    barrier = pltpu.get_barrier_semaphore()

    def greet(device):
        pl.semaphore_signal(barrier, inc=1, device_id=device, device_id_type=MESH)

    others(16, zz, lambda k, q: greet(of_z(q)))
    near = []
    count = jnp.int32(15 + 15 + 7 + 1)
    for a, b in STEPS:
        valid = (slab + a >= 0) & (slab + a < SLABS) & (cross + b >= 0) & (cross + b < CROSS)
        device = (lax.rem(slab + a + SLABS, SLABS), lax.rem(cross + b + CROSS, CROSS))
        near.append((valid, device))
        count += jnp.where(valid, 1, 0)

        @pl.when(valid)
        def _():
            greet(device)

    others(16, xy, lambda k, q: greet(of_xy(q)))
    others(8, xc, lambda k, q: greet(of_row(q)))
    greet(pair)

    fetches[0].wait()
    rows = vof_ref[...].astype(F32)
    for i in range(4):
        packed[HOME * i : HOME * i + HOME, :] = rows[:, 128 * i : 128 * i + 128]
    table[4] = packed[...].astype(BF16)

    pl.semaphore_wait(barrier, count)

    def halo_copy(k, slot, sem):
        return remote(table.at[4], table.at[slot], halo_s.at[k], halo_r.at[sem], near[k][1])

    def slot_of(a, b):
        return (1 + a) * 3 + 1 + b

    for k, (a, b) in enumerate(STEPS):

        @pl.when(near[k][0])
        def _():
            halo_copy(k, slot_of(-a, -b), STEPS.index((-a, -b))).start()

    fetches[7].wait()
    lane = lanes((8, 128))
    pick = pick_ref[...]
    pk[zhi] = jnp.where(
        lane < 64,
        jnp.broadcast_to(pick[:, 0:1], (8, 128)),
        jnp.broadcast_to(pick[:, 1:2], (8, 128)),
    )

    def row_copy(k, q, slot):
        return remote(extra, eb.at[slot], eb_s.at[k], eb_r.at[slot], of_row(q))

    def pick_copy(k, q, slot):
        return remote(pk.at[zhi], pk.at[slot], pk_s.at[k], pk_r.at[slot], of_hi(q))

    def out_copy(k, q, slot):
        return remote(ob.at[q], rb.at[slot], ob_s.at[k], ob_r.at[slot], of_hi(q))

    def xy_copy(k, q, slot):
        return remote(hs.at[q], rs.at[slot], rs_s.at[k], rs_r.at[slot], of_xy(q))

    def z_copy(k, q, slot):
        return remote(zb.at[zz], zb.at[slot], zb_s.at[k], zb_r.at[slot], of_z(q))

    def all_copy(k, q, slot):
        return remote(
            sum_ref.at[core, xy], sum_ref.at[core, slot], ag_s.at[k], ag_r.at[slot], of_xy(q)
        )

    def start(number, mine, copy):
        others(number, mine, lambda k, q: copy(k, q, mine).start())

    def arrive(number, mine, copy):
        others(number, mine, lambda k, q: copy(k, q, q).wait_recv())

    def sent(number, mine, copy):
        others(number, mine, lambda k, q: copy(k, q, mine).wait_send())

    start(4, zhi, pick_copy)

    fetches[1].wait()
    nbr = nbr_ref[...]
    device = (nbr * 43691) >> 19
    slot = nbr - 12 * device
    place = (((device >> 5) - slab + 1) * 3 + ((device & 31) - cross + 1)) * HOME + slot
    place = jnp.clip(place, 0, 9 * HOME - 1)
    lookup_vec[...] = jnp.where(nbr < 0, 9 * HOME, place)
    to_scalar = pltpu.make_async_copy(lookup_vec, lookup_ref, in_s.at[0])
    to_scalar.start()

    fetches[2].wait()
    build_first(w1_ref, w1p, t)
    fetches[3].wait()
    fetches[4].wait()
    for ref, i in ((bd2, 0), (bd3, 1)):
        ref[...] = jnp.zeros_like(ref)
        ref[0:128, 0:128] = wmid_ref[i]
        ref[128:256, 128:256] = wmid_ref[i]
    wl = wlast_ref[...].astype(F32)
    sub = lax.broadcasted_iota(jnp.int32, (128, 128), 0)
    for z in range(8):
        wle[:, 128 * z : 128 * z + 128] = jnp.where((sub & 7) == z, wl, 0.0).astype(BF16)
    fetches[5].wait()
    fetches[6].wait()
    source = target_ref[...].astype(F32)
    spread([source[:, 128 * i : 128 * i + 128] for i in range(4)], keep_in(tt), 8, 0)
    tab[9 * HOME] = jnp.zeros((8, 128), F32)

    def unpack(slot):
        packed[...] = table[slot].astype(F32)
        parts = [packed[HOME * i : HOME * i + HOME, :] for i in range(4)]
        spread(parts, keep_in(tall), 12, 2)
        for i in range(HOME):
            tab[HOME * slot + i] = tall[8 * i : 8 * i + 8, :]

    unpack(4)
    for k in reversed(range(8)):

        @pl.when(near[k][0])
        def _():
            halo_copy(k, slot_of(*STEPS[k]), k).wait_recv()

        unpack(slot_of(*STEPS[k]))

    to_scalar.wait()

    @pl.loop(0, HOME)
    def _(b):
        build_window(b, lookup_ref, tab, pad, xs)

    live = jnp.full((8, 128), live_ref[0], jnp.int32)

    def train(c):
        at = pl.ds(pl.multiple_of(c * CHUNK, CHUNK), CHUNK)
        window = xs[at, :]
        predicted = jnp.zeros((CHUNK, 128), F32)
        for j in range(4):
            col = slice(256 * j, 256 * j + 256)
            a = jnp.tanh(dot(window, t[:, col])).astype(BF16)
            h1[at, col] = a
            a = jnp.tanh(dot(a, bd2[...])).astype(BF16)
            h2[at, col] = a
            a = jnp.tanh(dot(a, bd3[...])).astype(BF16)
            h3[at, col] = a
            predicted += dot_n(a, wle[:, col])
        for i in range(CHUNK // 64):
            b = c * (CHUNK // 64) + i
            tile = jnp.zeros((8, 128), F32)
            for k in range(8):
                part = predicted[64 * i + 8 * k : 64 * i + 8 * k + 8]
                tile = jnp.where(((lane >> 3) & 7) == k, part, tile)
            rows = pl.ds(pl.multiple_of(b * 8, 8), 8)
            mask = jnp.where(b < live, 1.0, 0.0).astype(F32)
            pt[rows, :] = tile
            res = ((tile * mask - tt[rows, :]) * mask / SCALE).astype(BF16).astype(F32)
            for k in range(4):
                both = jnp.concatenate(
                    [
                        jnp.where((lane >> 3) == 2 * k, res, 0.0),
                        jnp.where((lane >> 3) == 2 * k + 1, res, 0.0),
                    ],
                    axis=0,
                )
                r2[pl.ds(pl.multiple_of(b * 64 + 16 * k, 16), 16), :] = both.astype(BF16)
        rr = r2[at, :]
        for j in range(4):
            col = slice(256 * j, 256 * j + 256)
            h = h3[at, col].astype(F32)
            d = (dot(rr, wle[:, col]) * (1.0 - h * h)).astype(BF16)
            d3[at, col] = d
            h = h2[at, col].astype(F32)
            d = (dot_n(d, bd3[...]) * (1.0 - h * h)).astype(BF16)
            d2[at, col] = d
            h = h1[at, col].astype(F32)
            d = (dot_n(d, bd2[...]) * (1.0 - h * h)).astype(BF16)
            d1[at, col] = d

    @pl.loop(0, 3)
    def _(c):
        train(2 - c)

        @pl.when(c == 1)
        def _():
            for i in range(3):
                at = 8 * (KEEP + 2 * i)
                extra[i] = jnp.where(lane < 64, pt[at : at + 8, :], pt[at + 8 : at + 16, :])
            eb[xc] = extra[...]
            start(8, xc, row_copy)

    second = jnp.zeros((128, 128), F32)
    third = jnp.zeros((128, 128), F32)
    for z in range(8):
        col = slice(128 * z, 128 * z + 128)
        second += dot_t(h1[:, col], d2[:, col])
        third += dot_t(h2[:, col], d3[:, col])
    flat[0:128, :] = second
    flat[128:256, :] = third

    arrive(4, zhi, pick_copy)
    arrive(8, xc, row_copy)
    ob[...] = jnp.zeros_like(ob)
    wants = [pk[q] for q in range(4)]

    @pl.loop(0, 8)
    def _(d):
        for i in range(3):
            tile = eb[d, i]
            swapped = shift(tile, 64)
            name = (zhi * 8 + d) * KEEP + 2 * i
            first = jnp.where(lane < 64, tile, swapped)
            other = jnp.where(lane < 64, swapped, tile)
            for q in range(4):
                old = ob[q]
                old = jnp.where(wants[q] == name, first, old)
                ob[q] = jnp.where(wants[q] == name + 1, other, old)

    start(4, zhi, out_copy)
    rb[zhi] = ob[zhi]

    total = jnp.zeros((WIN, 128), F32)
    xv = xs[...]
    for j in range(4):
        g = dot_t(xv, d1[:, 256 * j : 256 * j + 256])
        for i in range(2):
            z = 2 * j + i
            part = g[:, 128 * i : 128 * i + 128]
            total += part if z == 0 else pltpu.roll(part, WIN - z, 0)
    sums[...] = total
    for ax in range(5):
        for ay in range(5):
            at = 64 * ay + 12 * ax
            to = 256 + 25 * ax + 5 * ay
            flat[to : to + 5, :] = sums[at : at + 5, :]
    last = jnp.zeros((1, 128), F32)
    for j in range(4):
        g = dot_t(r2[...], h3[:, 256 * j : 256 * j + 256])
        for i in range(2):
            z = 2 * j + i
            part = jnp.where((sub & 7) == z, g[:, 128 * i : 128 * i + 128], 0.0)
            last += jnp.sum(part, axis=0, keepdims=True)
    flat[381:382, :] = last
    flat[382:384, :] = jnp.zeros((2, 128), F32)

    def half_of(c):
        return flat.at[pl.ds(pl.multiple_of(192 * c, 192), 192)]

    first_pair = remote(half_of(1 - core), cs, cs_s.at[0], cs_r.at[0], pair)
    first_pair.start()
    first_pair.wait_recv()
    half[...] = half_of(core)[...] + cs[...]
    for i in range(16):
        hs[i] = half[PIECE * i : PIECE * i + PIECE, :]
    start(16, xy, xy_copy)
    rs[xy] = hs[xy]
    arrive(16, xy, xy_copy)
    total = rs[0]
    for i in range(1, 16):
        total += rs[i]
    zb[zz] = total
    start(16, zz, z_copy)

    for b in range(KEEP):
        mask = jnp.where(b < live, 1.0, 0.0).astype(F32)
        pred_ref[8 * b : 8 * b + 8, :] = pt[8 * b : 8 * b + 8, :] * mask
    arrive(4, zhi, out_copy)
    tile = (rb[0] + rb[1]) + (rb[2] + rb[3])
    pred_ref[48:56, :] = tile
    pred_ref[56:64, :] = shift(tile, 64)

    for k in range(8):

        @pl.when(near[k][0])
        def _():
            halo_copy(k, 0, k).wait_send()

    sent(4, zhi, pick_copy)
    sent(8, xc, row_copy)
    sent(4, zhi, out_copy)
    first_pair.wait_send()
    sent(16, xy, xy_copy)

    arrive(16, zz, z_copy)
    total = zb[0]
    for i in range(1, 16):
        total += zb[i]
    sum_ref[core, xy] = total
    start(16, xy, all_copy)
    sent(16, zz, z_copy)
    arrive(16, xy, all_copy)
    last_pair = remote(sum_ref.at[core], sum_ref.at[core], cs_s.at[1], cs_r.at[1], pair)
    last_pair.start()
    sent(16, xy, all_copy)
    last_pair.wait_send()
    remote(
        sum_ref.at[1 - core], sum_ref.at[1 - core], cs_s.at[1], cs_r.at[1], pair
    ).wait_recv()


def write_kernel(sum_ref, tile_ref, pred_ref, gfirst_ref, gmid_ref, glast_ref, flat):
    for c in range(2):
        for i in range(16):
            at = 192 * c + PIECE * i
            flat[at : at + PIECE, :] = sum_ref[c, i]
    gmid_ref[0] = flat[0:128, :]
    gmid_ref[1] = flat[128:256, :]
    gfirst_ref[...] = flat[256:381, :]
    glast_ref[...] = flat[381:382, :]
    lane = lanes((8, 128))
    parts = [jnp.zeros((8, 128), F32) for _ in range(4)]
    for y in range(8):
        v = tile_ref[pl.ds(y, 8, stride=8), :]
        for x in range(8):
            low = 64 * (x % 2) + 8 * y
            inside = (lane >= low) & (lane < low + 8)
            parts[x // 2] = jnp.where(inside, shift(v, low - 8 * x), parts[x // 2])
    for i in range(4):
        pred_ref[:, 128 * i : 128 * i + 128] = parts[i]


def dma(n):
    return pltpu.SemaphoreType.DMA((n,))


def train(vof, target, neighbours, live_blocks, pick, w_first, w_mid, w_last):
    big = pltpu.VMEM((ROWS, 1024), BF16)
    piece = pltpu.VMEM((16, PIECE, 128), F32)
    tiles = pltpu.VMEM((4, 8, 128), F32)
    return pl.pallas_call(
        train_kernel,
        out_shape=(
            jax.ShapeDtypeStruct((2, 16, PIECE, 128), F32),
            jax.ShapeDtypeStruct((64, 128), F32),
        ),
        in_specs=[pl.BlockSpec(memory_space=pltpu.HBM)] * 8,
        out_specs=(VMEM, VMEM),
        scratch_shapes=[
            pltpu.VMEM((HOME, 512), BF16),
            pltpu.VMEM((HOME, 512), BF16),
            pltpu.VMEM((HOME, 26), jnp.int32),
            pltpu.SMEM((1,), jnp.int32),
            pltpu.VMEM((1, 2), jnp.int32),
            pltpu.VMEM((125, 128), BF16),
            pltpu.VMEM((2, 128, 128), BF16),
            pltpu.VMEM((1, 128), BF16),
            pltpu.VMEM((HOME, 26), jnp.int32),
            pltpu.SMEM((HOME, 26), jnp.int32),
            pltpu.VMEM((48, 128), F32),
            pltpu.VMEM((9, 48, 128), BF16),
            pltpu.VMEM((96, 128), F32),
            pltpu.VMEM((9 * HOME + 1, 8, 128), F32),
            pltpu.VMEM((96, 128), F32),
            pltpu.VMEM((2, 24, 128), F32),
            pltpu.VMEM((ROWS, WIN), BF16),
            pltpu.VMEM((128, 128), F32),
            pltpu.VMEM((WIN, 1024), BF16),
            pltpu.VMEM((256, 256), BF16),
            pltpu.VMEM((256, 256), BF16),
            pltpu.VMEM((128, 1024), BF16),
            big,
            big,
            big,
            big,
            big,
            big,
            pltpu.VMEM((ROWS, 128), BF16),
            pltpu.VMEM((96, 128), F32),
            pltpu.VMEM((384, 128), F32),
            pltpu.VMEM((384, 128), F32),
            pltpu.VMEM((3, 8, 128), F32),
            pltpu.VMEM((8, 3, 8, 128), F32),
            pltpu.VMEM((4, 8, 128), jnp.int32),
            tiles,
            tiles,
            pltpu.VMEM((192, 128), F32),
            pltpu.VMEM((192, 128), F32),
            piece,
            piece,
            piece,
            dma(8),
            dma(8),
            dma(8),
            dma(8),
            dma(8),
            dma(4),
            dma(4),
            dma(4),
            dma(4),
            dma(2),
            dma(2),
            dma(16),
            dma(16),
            dma(16),
            dma(16),
            dma(16),
            dma(16),
        ],
        compiler_params=pltpu.CompilerParams(
            collective_id=0, has_side_effects=True, vmem_limit_bytes=63 << 20
        ),
        name="train",
    )(vof, target, neighbours, live_blocks, pick, w_first, w_mid, w_last)


def shards(vof, target, neighbours, live_blocks, pick, w_first, w_mid, w_last):
    sums, tiles = train(
        vof,
        target,
        neighbours,
        live_blocks,
        pick,
        w_first,
        w_mid,
        w_last.reshape(1, 128),
    )
    pred, gfirst, gmid, glast = pl.pallas_call(
        write_kernel,
        out_shape=(
            jax.ShapeDtypeStruct((8, 512), F32),
            jax.ShapeDtypeStruct((125, 128), F32),
            jax.ShapeDtypeStruct((2, 128, 128), F32),
            jax.ShapeDtypeStruct((1, 128), F32),
        ),
        in_specs=[VMEM, VMEM],
        out_specs=(VMEM, VMEM, VMEM, VMEM),
        scratch_shapes=[pltpu.VMEM((384, 128), F32)],
        name="write",
    )(sums, tiles)
    return pred, gfirst, gmid, glast.reshape(128)


def solution(mesh):
    both = ("stream", "cross")
    return jax.shard_map(
        shards,
        mesh=mesh,
        in_specs=(
            P(both, None),
            P(both, None),
            P(both, None),
            P(both),
            P(both, None),
            P(),
            P(),
            P(),
        ),
        out_specs=(P(both, None), P(), P(), P()),
        check_vma=False,
    )
```

```python
import jax
import jax.numpy as jnp
from jax import lax
from jax.experimental import pallas as pl
from jax.experimental.pallas import tpu as pltpu
from jax.sharding import PartitionSpec as P

MESH = pl.DeviceIdType.MESH
F32 = jnp.float32
BF16 = jnp.bfloat16

KEEP = 6
HOME = 12
ROWS = 768
WIN = 384
SCALE = 1572864.0
SLABS = 16
CROSS = 32
PIECE = 12
VMEM = pl.BlockSpec(memory_space=pltpu.VMEM)


def lanes(shape):
    return lax.broadcasted_iota(jnp.int32, shape, len(shape) - 1)


def shift(x, by):
    by = by % 128
    return x if by == 0 else pltpu.roll(x, by, x.ndim - 1)


def spread(parts, store, stride, first):
    lane = lanes(parts[0].shape)
    for y in range(8):
        total = jnp.zeros_like(parts[0])
        for x in range(8):
            moved = shift(parts[x // 2], stride * x + first - (64 * (x % 2) + 8 * y))
            low = stride * x + first
            total = jnp.where((lane >= low) & (lane < low + 8), moved, total)
        store(y, total)


def keep_in(ref):
    def store(y, tile):
        ref[pl.ds(y, HOME, stride=8), :] = tile

    return store


def remote(src, dst, send, recv, device):
    return pltpu.make_async_remote_copy(
        src_ref=src,
        dst_ref=dst,
        send_sem=send,
        recv_sem=recv,
        device_id=device,
        device_id_type=MESH,
    )


def dot_t(a, b):
    return lax.dot_general(a, b, (((0,), (0,)), ((), ())), preferred_element_type=F32)


def dot_n(a, b):
    return lax.dot_general(a, b, (((1,), (1,)), ((), ())), preferred_element_type=F32)


def dot(a, b):
    return jnp.dot(a, b, preferred_element_type=F32)


def build_first(w1_ref, w1p, t):
    w1p[...] = jnp.zeros_like(w1p)
    w1p[0:125, :] = w1_ref[...].astype(F32)
    w1 = w1p[...].astype(BF16)
    k = lax.broadcasted_iota(jnp.int32, (WIN, 128), 0)
    f = lanes((WIN, 128))
    m = k & 63
    ax = (m * 43) >> 9
    zp = m - 12 * ax
    ay = k >> 6
    code = jnp.where((m < 60) & (ay < 5), 25 * ax + 5 * ay + zp, -1000)
    for z in range(8):
        hit = (f == code - z) & (zp >= z) & (zp < z + 5)
        select = jnp.where(hit, 1.0, 0.0).astype(BF16)
        t[:, 128 * z : 128 * z + 128] = dot(select, w1).astype(BF16)


def build_window(b, lookup_ref, tab, pad, xs):
    lane = lanes((8, 128))
    zp = lane - 12 * ((lane * 43) >> 9)
    for dy in range(3):
        row = []
        for dx in range(3):
            got = []
            for dz in range(3):
                k = 9 * dx + 3 * dy + dz
                if k == 13:
                    at = 4 * HOME + b
                else:
                    at = lookup_ref[b, k if k < 13 else k - 1]
                got.append(tab[at])
            row.append(
                jnp.where(zp < 2, shift(got[0], -8), jnp.where(zp < 10, got[1], shift(got[2], 8)))
            )
        low = jnp.where(lane < 24, shift(row[0], -72), shift(row[1], 24))
        high = jnp.where(lane < 72, shift(row[1], -24), shift(row[2], 72))
        pad[2 * b, 8 * dy : 8 * dy + 8, :] = low
        pad[2 * b + 1, 8 * dy : 8 * dy + 8, :] = high
    for half in range(2):
        a = [pad[2 * b + half, 6 + ay : 14 + ay, :] for ay in range(5)]
        odd = [shift(a[1], 64), shift(a[3], 64)]
        made = []
        for x in range(4):
            inside = (lane >= 12 * x) & (lane < 12 * x + 64)
            made.append(
                [
                    shift(jnp.where(inside, a[0], odd[0]), -12 * x),
                    shift(jnp.where(inside, a[2], odd[1]), -12 * x),
                    shift(a[4], -12 * x),
                ]
            )
        for pair in range(2):
            for g in range(3):
                both = jnp.concatenate([made[2 * pair][g], made[2 * pair + 1][g]], axis=0)
                base = 64 * b + 32 * half + 16 * pair
                xs[base : base + 16, 128 * g : 128 * g + 128] = both.astype(BF16)


STEPS = [(a, b) for a in (-1, 0, 1) for b in (-1, 0, 1) if (a, b) != (0, 0)]
STEPS.sort(key=lambda step: (step[1] == 0, step[0] == 0))


def train_kernel(
    vof_hbm,
    target_hbm,
    nbr_hbm,
    live_hbm,
    pick_hbm,
    w1_hbm,
    wmid_hbm,
    wlast_hbm,
    sum_ref,
    pred_ref,
    vof_ref,
    target_ref,
    nbr_ref,
    live_ref,
    pick_ref,
    w1_ref,
    wmid_ref,
    wlast_ref,
    lookup_vec,
    lookup_ref,
    packed,
    table,
    tall,
    tab,
    tt,
    pad,
    xs,
    w1p,
    t,
    bd2,
    bd3,
    wle,
    h1,
    h2,
    h3,
    d1,
    d2,
    d3,
    r2,
    pt,
    flat,
    sums,
    extra,
    eb,
    pk,
    ob,
    rb,
    cs,
    half,
    hs,
    rs,
    zb,
    in_s,
    halo_s,
    halo_r,
    eb_s,
    eb_r,
    pk_s,
    pk_r,
    ob_s,
    ob_r,
    cs_s,
    cs_r,
    rs_s,
    rs_r,
    zb_s,
    zb_r,
    ag_s,
    ag_r,
):
    fetches = [
        pltpu.make_async_copy(src, dst, in_s.at[i])
        for i, (src, dst) in enumerate(
            (
                (vof_hbm, vof_ref),
                (nbr_hbm, nbr_ref),
                (w1_hbm, w1_ref),
                (wmid_hbm, wmid_ref),
                (wlast_hbm, wlast_ref),
                (target_hbm, target_ref),
                (live_hbm, live_ref),
                (pick_hbm, pick_ref),
            )
        )
    ]
    for fetch in fetches:
        fetch.start()

    slab = lax.axis_index("stream")
    cross = lax.axis_index("cross")
    zlo, y = slab // 4, lax.rem(slab, 4)
    zhi, xc = cross // 8, lax.rem(cross, 8)
    x, core = xc // 2, lax.rem(xc, 2)
    zz = zhi * 4 + zlo
    xy = y * 4 + x
    pair = (slab, cross + 1 - 2 * core)

    def of_xy(q):
        return (zlo * 4 + q // 4, zhi * 8 + 2 * lax.rem(q, 4) + core)

    def of_z(q):
        return (lax.rem(q, 4) * 4 + y, (q // 4) * 8 + xc)

    def of_hi(q):
        return (slab, q * 8 + xc)

    def of_row(q):
        return (slab, zhi * 8 + q)

    def others(number, mine, body):
        def step(k, carry):
            body(k, lax.rem(mine + k, number))
            return carry

        lax.fori_loop(1, number, step, 0)

    table[...] = jnp.zeros_like(table)

    barrier = pltpu.get_barrier_semaphore()

    def greet(device):
        pl.semaphore_signal(barrier, inc=1, device_id=device, device_id_type=MESH)

    others(16, zz, lambda k, q: greet(of_z(q)))
    near = []
    count = jnp.int32(15 + 15 + 7 + 1)
    for a, b in STEPS:
        valid = (slab + a >= 0) & (slab + a < SLABS) & (cross + b >= 0) & (cross + b < CROSS)
        device = (lax.rem(slab + a + SLABS, SLABS), lax.rem(cross + b + CROSS, CROSS))
        near.append((valid, device))
        count += jnp.where(valid, 1, 0)

        @pl.when(valid)
        def _():
            greet(device)

    others(16, xy, lambda k, q: greet(of_xy(q)))
    others(8, xc, lambda k, q: greet(of_row(q)))
    greet(pair)

    fetches[0].wait()
    rows = vof_ref[...].astype(F32)
    for i in range(4):
        packed[HOME * i : HOME * i + HOME, :] = rows[:, 128 * i : 128 * i + 128]
    table[4] = packed[...].astype(BF16)

    pl.semaphore_wait(barrier, count)

    def halo_copy(k, slot, sem):
        return remote(table.at[4], table.at[slot], halo_s.at[k], halo_r.at[sem], near[k][1])

    def slot_of(a, b):
        return (1 + a) * 3 + 1 + b

    for k, (a, b) in enumerate(STEPS):

        @pl.when(near[k][0])
        def _():
            halo_copy(k, slot_of(-a, -b), STEPS.index((-a, -b))).start()

    fetches[7].wait()
    lane = lanes((8, 128))
    pick = pick_ref[...]
    pk[zhi] = jnp.where(
        lane < 64,
        jnp.broadcast_to(pick[:, 0:1], (8, 128)),
        jnp.broadcast_to(pick[:, 1:2], (8, 128)),
    )

    def row_copy(k, q, slot):
        return remote(extra, eb.at[slot], eb_s.at[k], eb_r.at[slot], of_row(q))

    def pick_copy(k, q, slot):
        return remote(pk.at[zhi], pk.at[slot], pk_s.at[k], pk_r.at[slot], of_hi(q))

    def out_copy(k, q, slot):
        return remote(ob.at[q], rb.at[slot], ob_s.at[k], ob_r.at[slot], of_hi(q))

    def xy_copy(k, q, slot):
        return remote(hs.at[q], rs.at[slot], rs_s.at[k], rs_r.at[slot], of_xy(q))

    def z_copy(k, q, slot):
        return remote(zb.at[zz], zb.at[slot], zb_s.at[k], zb_r.at[slot], of_z(q))

    def all_copy(k, q, slot):
        return remote(
            sum_ref.at[core, xy], sum_ref.at[core, slot], ag_s.at[k], ag_r.at[slot], of_xy(q)
        )

    def start(number, mine, copy):
        others(number, mine, lambda k, q: copy(k, q, mine).start())

    def arrive(number, mine, copy):
        others(number, mine, lambda k, q: copy(k, q, q).wait_recv())

    def sent(number, mine, copy):
        others(number, mine, lambda k, q: copy(k, q, mine).wait_send())

    start(4, zhi, pick_copy)

    fetches[1].wait()
    nbr = nbr_ref[...]
    device = (nbr * 43691) >> 19
    slot = nbr - 12 * device
    place = (((device >> 5) - slab + 1) * 3 + ((device & 31) - cross + 1)) * HOME + slot
    place = jnp.clip(place, 0, 9 * HOME - 1)
    lookup_vec[...] = jnp.where(nbr < 0, 9 * HOME, place)
    to_scalar = pltpu.make_async_copy(lookup_vec, lookup_ref, in_s.at[0])
    to_scalar.start()

    fetches[2].wait()
    build_first(w1_ref, w1p, t)
    fetches[3].wait()
    fetches[4].wait()
    for ref, i in ((bd2, 0), (bd3, 1)):
        ref[...] = jnp.zeros_like(ref)
        ref[0:128, 0:128] = wmid_ref[i]
        ref[128:256, 128:256] = wmid_ref[i]
    wl = wlast_ref[...].astype(F32)
    sub = lax.broadcasted_iota(jnp.int32, (128, 128), 0)
    for z in range(8):
        wle[:, 128 * z : 128 * z + 128] = jnp.where((sub & 7) == z, wl, 0.0).astype(BF16)
    fetches[5].wait()
    fetches[6].wait()
    source = target_ref[...].astype(F32)
    spread([source[:, 128 * i : 128 * i + 128] for i in range(4)], keep_in(tt), 8, 0)
    tab[9 * HOME] = jnp.zeros((8, 128), F32)

    def unpack(slot):
        packed[...] = table[slot].astype(F32)
        parts = [packed[HOME * i : HOME * i + HOME, :] for i in range(4)]
        spread(parts, keep_in(tall), 12, 2)
        for i in range(HOME):
            tab[HOME * slot + i] = tall[8 * i : 8 * i + 8, :]

    unpack(4)
    for k in reversed(range(8)):

        @pl.when(near[k][0])
        def _():
            halo_copy(k, slot_of(*STEPS[k]), k).wait_recv()

        unpack(slot_of(*STEPS[k]))

    to_scalar.wait()

    for b in range(HOME):
        build_window(b, lookup_ref, tab, pad, xs)

    live = jnp.full((8, 128), live_ref[0], jnp.int32)

    window = xs[...]
    predicted = jnp.zeros((ROWS, 128), F32)
    for j in range(4):
        col = slice(256 * j, 256 * j + 256)
        a = jnp.tanh(dot(window, t[:, col])).astype(BF16)
        h1[:, col] = a
        a = jnp.tanh(dot(a, bd2[...])).astype(BF16)
        h2[:, col] = a
        a = jnp.tanh(dot(a, bd3[...])).astype(BF16)
        h3[:, col] = a
        predicted += dot_n(a, wle[:, col])
    for b in range(HOME):
        tile = jnp.zeros((8, 128), F32)
        for k in range(8):
            part = predicted[64 * b + 8 * k : 64 * b + 8 * k + 8]
            tile = jnp.where(((lane >> 3) & 7) == k, part, tile)
        pt[8 * b : 8 * b + 8, :] = tile
    for i in range(3):
        at = 8 * (KEEP + 2 * i)
        extra[i] = jnp.where(lane < 64, pt[at : at + 8, :], pt[at + 8 : at + 16, :])
    eb[xc] = extra[...]
    start(8, xc, row_copy)
    for b in range(HOME):
        rows = slice(8 * b, 8 * b + 8)
        mask = jnp.where(b < live, 1.0, 0.0).astype(F32)
        res = ((pt[rows, :] * mask - tt[rows, :]) * mask / SCALE).astype(BF16).astype(F32)
        for k in range(4):
            both = jnp.concatenate(
                [
                    jnp.where((lane >> 3) == 2 * k, res, 0.0),
                    jnp.where((lane >> 3) == 2 * k + 1, res, 0.0),
                ],
                axis=0,
            )
            r2[64 * b + 16 * k : 64 * b + 16 * k + 16, :] = both.astype(BF16)
    rr = r2[...]
    for j in range(4):
        col = slice(256 * j, 256 * j + 256)
        h = h3[:, col].astype(F32)
        d = (dot(rr, wle[:, col]) * (1.0 - h * h)).astype(BF16)
        d3[:, col] = d
        h = h2[:, col].astype(F32)
        d = (dot_n(d, bd3[...]) * (1.0 - h * h)).astype(BF16)
        d2[:, col] = d
        h = h1[:, col].astype(F32)
        d = (dot_n(d, bd2[...]) * (1.0 - h * h)).astype(BF16)
        d1[:, col] = d

    second = jnp.zeros((128, 128), F32)
    third = jnp.zeros((128, 128), F32)
    for z in range(8):
        col = slice(128 * z, 128 * z + 128)
        second += dot_t(h1[:, col], d2[:, col])
        third += dot_t(h2[:, col], d3[:, col])
    flat[0:128, :] = second
    flat[128:256, :] = third

    arrive(4, zhi, pick_copy)
    arrive(8, xc, row_copy)
    ob[...] = jnp.zeros_like(ob)
    wants = [pk[q] for q in range(4)]

    @pl.loop(0, 8)
    def _(d):
        for i in range(3):
            tile = eb[d, i]
            swapped = shift(tile, 64)
            name = (zhi * 8 + d) * KEEP + 2 * i
            first = jnp.where(lane < 64, tile, swapped)
            other = jnp.where(lane < 64, swapped, tile)
            for q in range(4):
                old = ob[q]
                old = jnp.where(wants[q] == name, first, old)
                ob[q] = jnp.where(wants[q] == name + 1, other, old)

    start(4, zhi, out_copy)
    rb[zhi] = ob[zhi]

    total = jnp.zeros((WIN, 128), F32)
    xv = xs[...]
    for j in range(4):
        g = dot_t(xv, d1[:, 256 * j : 256 * j + 256])
        for i in range(2):
            z = 2 * j + i
            part = g[:, 128 * i : 128 * i + 128]
            total += part if z == 0 else pltpu.roll(part, WIN - z, 0)
    sums[...] = total
    for ax in range(5):
        for ay in range(5):
            at = 64 * ay + 12 * ax
            to = 256 + 25 * ax + 5 * ay
            flat[to : to + 5, :] = sums[at : at + 5, :]
    last = jnp.zeros((1, 128), F32)
    for j in range(4):
        g = dot_t(r2[...], h3[:, 256 * j : 256 * j + 256])
        for i in range(2):
            z = 2 * j + i
            part = jnp.where((sub & 7) == z, g[:, 128 * i : 128 * i + 128], 0.0)
            last += jnp.sum(part, axis=0, keepdims=True)
    flat[381:382, :] = last
    flat[382:384, :] = jnp.zeros((2, 128), F32)

    def half_of(c):
        return flat.at[pl.ds(pl.multiple_of(192 * c, 192), 192)]

    first_pair = remote(half_of(1 - core), cs, cs_s.at[0], cs_r.at[0], pair)
    first_pair.start()
    first_pair.wait_recv()
    half[...] = half_of(core)[...] + cs[...]
    for i in range(16):
        hs[i] = half[PIECE * i : PIECE * i + PIECE, :]
    start(16, xy, xy_copy)
    rs[xy] = hs[xy]
    arrive(16, xy, xy_copy)
    total = rs[0]
    for i in range(1, 16):
        total += rs[i]
    zb[zz] = total
    start(16, zz, z_copy)

    for b in range(KEEP):
        mask = jnp.where(b < live, 1.0, 0.0).astype(F32)
        pred_ref[8 * b : 8 * b + 8, :] = pt[8 * b : 8 * b + 8, :] * mask
    arrive(4, zhi, out_copy)
    tile = (rb[0] + rb[1]) + (rb[2] + rb[3])
    pred_ref[48:56, :] = tile
    pred_ref[56:64, :] = shift(tile, 64)

    for k in range(8):

        @pl.when(near[k][0])
        def _():
            halo_copy(k, 0, k).wait_send()

    sent(4, zhi, pick_copy)
    sent(8, xc, row_copy)
    sent(4, zhi, out_copy)
    first_pair.wait_send()
    sent(16, xy, xy_copy)

    arrive(16, zz, z_copy)
    total = zb[0]
    for i in range(1, 16):
        total += zb[i]
    sum_ref[core, xy] = total
    start(16, xy, all_copy)
    sent(16, zz, z_copy)
    arrive(16, xy, all_copy)
    last_pair = remote(sum_ref.at[core], sum_ref.at[core], cs_s.at[1], cs_r.at[1], pair)
    last_pair.start()
    sent(16, xy, all_copy)
    last_pair.wait_send()
    remote(
        sum_ref.at[1 - core], sum_ref.at[1 - core], cs_s.at[1], cs_r.at[1], pair
    ).wait_recv()


def write_kernel(sum_ref, tile_ref, pred_ref, gfirst_ref, gmid_ref, glast_ref, flat):
    for c in range(2):
        for i in range(16):
            at = 192 * c + PIECE * i
            flat[at : at + PIECE, :] = sum_ref[c, i]
    gmid_ref[0] = flat[0:128, :]
    gmid_ref[1] = flat[128:256, :]
    gfirst_ref[...] = flat[256:381, :]
    glast_ref[...] = flat[381:382, :]
    lane = lanes((8, 128))
    parts = [jnp.zeros((8, 128), F32) for _ in range(4)]
    for y in range(8):
        v = tile_ref[pl.ds(y, 8, stride=8), :]
        for x in range(8):
            low = 64 * (x % 2) + 8 * y
            inside = (lane >= low) & (lane < low + 8)
            parts[x // 2] = jnp.where(inside, shift(v, low - 8 * x), parts[x // 2])
    for i in range(4):
        pred_ref[:, 128 * i : 128 * i + 128] = parts[i]


def dma(n):
    return pltpu.SemaphoreType.DMA((n,))


def train(vof, target, neighbours, live_blocks, pick, w_first, w_mid, w_last):
    big = pltpu.VMEM((ROWS, 1024), BF16)
    piece = pltpu.VMEM((16, PIECE, 128), F32)
    tiles = pltpu.VMEM((4, 8, 128), F32)
    return pl.pallas_call(
        train_kernel,
        out_shape=(
            jax.ShapeDtypeStruct((2, 16, PIECE, 128), F32),
            jax.ShapeDtypeStruct((64, 128), F32),
        ),
        in_specs=[pl.BlockSpec(memory_space=pltpu.HBM)] * 8,
        out_specs=(VMEM, VMEM),
        scratch_shapes=[
            pltpu.VMEM((HOME, 512), BF16),
            pltpu.VMEM((HOME, 512), BF16),
            pltpu.VMEM((HOME, 26), jnp.int32),
            pltpu.SMEM((1,), jnp.int32),
            pltpu.VMEM((1, 2), jnp.int32),
            pltpu.VMEM((125, 128), BF16),
            pltpu.VMEM((2, 128, 128), BF16),
            pltpu.VMEM((1, 128), BF16),
            pltpu.VMEM((HOME, 26), jnp.int32),
            pltpu.SMEM((HOME, 26), jnp.int32),
            pltpu.VMEM((48, 128), F32),
            pltpu.VMEM((9, 48, 128), BF16),
            pltpu.VMEM((96, 128), F32),
            pltpu.VMEM((9 * HOME + 1, 8, 128), F32),
            pltpu.VMEM((96, 128), F32),
            pltpu.VMEM((2 * HOME, 24, 128), F32),
            pltpu.VMEM((ROWS, WIN), BF16),
            pltpu.VMEM((128, 128), F32),
            pltpu.VMEM((WIN, 1024), BF16),
            pltpu.VMEM((256, 256), BF16),
            pltpu.VMEM((256, 256), BF16),
            pltpu.VMEM((128, 1024), BF16),
            big,
            big,
            big,
            big,
            big,
            big,
            pltpu.VMEM((ROWS, 128), BF16),
            pltpu.VMEM((96, 128), F32),
            pltpu.VMEM((384, 128), F32),
            pltpu.VMEM((384, 128), F32),
            pltpu.VMEM((3, 8, 128), F32),
            pltpu.VMEM((8, 3, 8, 128), F32),
            pltpu.VMEM((4, 8, 128), jnp.int32),
            tiles,
            tiles,
            pltpu.VMEM((192, 128), F32),
            pltpu.VMEM((192, 128), F32),
            piece,
            piece,
            piece,
            dma(8),
            dma(8),
            dma(8),
            dma(8),
            dma(8),
            dma(4),
            dma(4),
            dma(4),
            dma(4),
            dma(2),
            dma(2),
            dma(16),
            dma(16),
            dma(16),
            dma(16),
            dma(16),
            dma(16),
        ],
        compiler_params=pltpu.CompilerParams(
            collective_id=0, has_side_effects=True, vmem_limit_bytes=63 << 20
        ),
        name="train",
    )(vof, target, neighbours, live_blocks, pick, w_first, w_mid, w_last)


def shards(vof, target, neighbours, live_blocks, pick, w_first, w_mid, w_last):
    sums, tiles = train(
        vof,
        target,
        neighbours,
        live_blocks,
        pick,
        w_first,
        w_mid,
        w_last.reshape(1, 128),
    )
    pred, gfirst, gmid, glast = pl.pallas_call(
        write_kernel,
        out_shape=(
            jax.ShapeDtypeStruct((8, 512), F32),
            jax.ShapeDtypeStruct((125, 128), F32),
            jax.ShapeDtypeStruct((2, 128, 128), F32),
            jax.ShapeDtypeStruct((1, 128), F32),
        ),
        in_specs=[VMEM, VMEM],
        out_specs=(VMEM, VMEM, VMEM, VMEM),
        scratch_shapes=[pltpu.VMEM((384, 128), F32)],
        name="write",
    )(sums, tiles)
    return pred, gfirst, gmid, glast.reshape(128)


def solution(mesh):
    both = ("stream", "cross")
    return jax.shard_map(
        shards,
        mesh=mesh,
        in_specs=(
            P(both, None),
            P(both, None),
            P(both, None),
            P(both),
            P(both, None),
            P(),
            P(),
            P(),
        ),
        out_specs=(P(both, None), P(), P(), P()),
        check_vma=False,
    )
```

```python
import jax
import jax.numpy as jnp
from jax import lax
from jax.experimental import pallas as pl
from jax.experimental.pallas import tpu as pltpu
from jax.sharding import PartitionSpec as P

MESH = pl.DeviceIdType.MESH
F32 = jnp.float32
BF16 = jnp.bfloat16

KEEP = 6
HOME = 12
ROWS = 768
WIN = 384
SCALE = 1572864.0
SLABS = 16
CROSS = 32
PIECE = 12
VMEM = pl.BlockSpec(memory_space=pltpu.VMEM)


def lanes(shape):
    return lax.broadcasted_iota(jnp.int32, shape, len(shape) - 1)


def shift(x, by):
    by = by % 128
    return x if by == 0 else pltpu.roll(x, by, x.ndim - 1)


def spread(parts, store, stride, first):
    lane = lanes(parts[0].shape)
    for y in range(8):
        total = jnp.zeros_like(parts[0])
        for x in range(8):
            moved = shift(parts[x // 2], stride * x + first - (64 * (x % 2) + 8 * y))
            low = stride * x + first
            total = jnp.where((lane >= low) & (lane < low + 8), moved, total)
        store(y, total)


def keep_in(ref):
    def store(y, tile):
        ref[pl.ds(y, HOME, stride=8), :] = tile

    return store


def remote(src, dst, send, recv, device):
    return pltpu.make_async_remote_copy(
        src_ref=src,
        dst_ref=dst,
        send_sem=send,
        recv_sem=recv,
        device_id=device,
        device_id_type=MESH,
    )


def dot_t(a, b):
    return lax.dot_general(a, b, (((0,), (0,)), ((), ())), preferred_element_type=F32)


def dot_n(a, b):
    return lax.dot_general(a, b, (((1,), (1,)), ((), ())), preferred_element_type=F32)


def dot(a, b):
    return jnp.dot(a, b, preferred_element_type=F32)


def build_first(w1_ref, w1p, t):
    w1p[...] = jnp.zeros_like(w1p)
    w1p[0:125, :] = w1_ref[...].astype(F32)
    w1 = w1p[...].astype(BF16)
    k = lax.broadcasted_iota(jnp.int32, (WIN, 128), 0)
    f = lanes((WIN, 128))
    m = k & 63
    ax = (m * 43) >> 9
    zp = m - 12 * ax
    ay = k >> 6
    code = jnp.where((m < 60) & (ay < 5), 25 * ax + 5 * ay + zp, -1000)
    for z in range(8):
        hit = (f == code - z) & (zp >= z) & (zp < z + 5)
        select = jnp.where(hit, 1.0, 0.0).astype(BF16)
        t[:, 128 * z : 128 * z + 128] = dot(select, w1).astype(BF16)


def build_window(b, lookup_ref, tab, pad, xs):
    lane = lanes((8, 128))
    zp = lane - 12 * ((lane * 43) >> 9)
    for dy in range(3):
        row = []
        for dx in range(3):
            got = []
            for dz in range(3):
                k = 9 * dx + 3 * dy + dz
                if k == 13:
                    at = 4 * HOME + b
                else:
                    at = lookup_ref[b, k if k < 13 else k - 1]
                got.append(tab[at])
            row.append(
                jnp.where(zp < 2, shift(got[0], -8), jnp.where(zp < 10, got[1], shift(got[2], 8)))
            )
        low = jnp.where(lane < 24, shift(row[0], -72), shift(row[1], 24))
        high = jnp.where(lane < 72, shift(row[1], -24), shift(row[2], 72))
        pad[2 * b, 8 * dy : 8 * dy + 8, :] = low
        pad[2 * b + 1, 8 * dy : 8 * dy + 8, :] = high
    for half in range(2):
        a = [pad[2 * b + half, 6 + ay : 14 + ay, :] for ay in range(5)]
        odd = [shift(a[1], 64), shift(a[3], 64)]
        made = []
        for x in range(4):
            inside = (lane >= 12 * x) & (lane < 12 * x + 64)
            made.append(
                [
                    shift(jnp.where(inside, a[0], odd[0]), -12 * x),
                    shift(jnp.where(inside, a[2], odd[1]), -12 * x),
                    shift(a[4], -12 * x),
                ]
            )
        for pair in range(2):
            for g in range(3):
                both = jnp.concatenate([made[2 * pair][g], made[2 * pair + 1][g]], axis=0)
                base = 64 * b + 32 * half + 16 * pair
                xs[base : base + 16, 128 * g : 128 * g + 128] = both.astype(BF16)


STEPS = [(a, b) for a in (-1, 0, 1) for b in (-1, 0, 1) if (a, b) != (0, 0)]
STEPS.sort(key=lambda step: (step[1] == 0, step[0] == 0))


def train_kernel(
    vof_hbm,
    target_hbm,
    nbr_hbm,
    live_hbm,
    pick_hbm,
    w1_hbm,
    wmid_hbm,
    wlast_hbm,
    sum_ref,
    pred_ref,
    vof_ref,
    target_ref,
    nbr_ref,
    live_ref,
    pick_ref,
    w1_ref,
    wmid_ref,
    wlast_ref,
    lookup_vec,
    lookup_ref,
    packed,
    table,
    tab,
    tt,
    pad,
    xs,
    w1p,
    t,
    bd2,
    bd3,
    wle,
    h1,
    h2,
    h3,
    d1,
    d2,
    d3,
    r2,
    pt,
    flat,
    sums,
    extra,
    eb,
    pk,
    ob,
    rb,
    cs,
    half,
    hs,
    rs,
    zb,
    in_s,
    halo_s,
    halo_r,
    eb_s,
    eb_r,
    pk_s,
    pk_r,
    ob_s,
    ob_r,
    cs_s,
    cs_r,
    rs_s,
    rs_r,
    zb_s,
    zb_r,
    ag_s,
    ag_r,
):
    fetches = [
        pltpu.make_async_copy(src, dst, in_s.at[i])
        for i, (src, dst) in enumerate(
            (
                (vof_hbm, vof_ref),
                (nbr_hbm, nbr_ref),
                (w1_hbm, w1_ref),
                (wmid_hbm, wmid_ref),
                (wlast_hbm, wlast_ref),
                (target_hbm, target_ref),
                (live_hbm, live_ref),
                (pick_hbm, pick_ref),
            )
        )
    ]
    for fetch in fetches:
        fetch.start()

    slab = lax.axis_index("stream")
    cross = lax.axis_index("cross")
    zlo, y = slab // 4, lax.rem(slab, 4)
    zhi, xc = cross // 8, lax.rem(cross, 8)
    x, core = xc // 2, lax.rem(xc, 2)
    zz = zhi * 4 + zlo
    xy = y * 4 + x
    pair = (slab, cross + 1 - 2 * core)

    def of_xy(q):
        return (zlo * 4 + q // 4, zhi * 8 + 2 * lax.rem(q, 4) + core)

    def of_z(q):
        return (lax.rem(q, 4) * 4 + y, (q // 4) * 8 + xc)

    def of_hi(q):
        return (slab, q * 8 + xc)

    def of_row(q):
        return (slab, zhi * 8 + q)

    def others(number, mine, body):
        def step(k, carry):
            body(k, lax.rem(mine + k, number))
            return carry

        lax.fori_loop(1, number, step, 0)

    table[...] = jnp.zeros_like(table)

    barrier = pltpu.get_barrier_semaphore()

    def greet(device):
        pl.semaphore_signal(barrier, inc=1, device_id=device, device_id_type=MESH)

    others(16, zz, lambda k, q: greet(of_z(q)))
    near = []
    count = jnp.int32(15 + 15 + 7 + 1)
    for a, b in STEPS:
        valid = (slab + a >= 0) & (slab + a < SLABS) & (cross + b >= 0) & (cross + b < CROSS)
        device = (lax.rem(slab + a + SLABS, SLABS), lax.rem(cross + b + CROSS, CROSS))
        near.append((valid, device))
        count += jnp.where(valid, 1, 0)

        @pl.when(valid)
        def _():
            greet(device)

    others(16, xy, lambda k, q: greet(of_xy(q)))
    others(8, xc, lambda k, q: greet(of_row(q)))
    greet(pair)

    fetches[0].wait()
    rows = vof_ref[...].astype(F32)
    for i in range(4):
        packed[4, HOME * i : HOME * i + HOME, :] = rows[:, 128 * i : 128 * i + 128]
    table[4] = packed[4].astype(BF16)

    pl.semaphore_wait(barrier, count)

    def halo_copy(k, slot, sem):
        return remote(table.at[4], table.at[slot], halo_s.at[k], halo_r.at[sem], near[k][1])

    def slot_of(a, b):
        return (1 + a) * 3 + 1 + b

    for k, (a, b) in enumerate(STEPS):

        @pl.when(near[k][0])
        def _():
            halo_copy(k, slot_of(-a, -b), STEPS.index((-a, -b))).start()

    fetches[7].wait()
    lane = lanes((8, 128))
    pick = pick_ref[...]
    pk[zhi] = jnp.where(
        lane < 64,
        jnp.broadcast_to(pick[:, 0:1], (8, 128)),
        jnp.broadcast_to(pick[:, 1:2], (8, 128)),
    )

    def row_copy(k, q, slot):
        return remote(extra, eb.at[slot], eb_s.at[k], eb_r.at[slot], of_row(q))

    def pick_copy(k, q, slot):
        return remote(pk.at[zhi], pk.at[slot], pk_s.at[k], pk_r.at[slot], of_hi(q))

    def out_copy(k, q, slot):
        return remote(ob.at[q], rb.at[slot], ob_s.at[k], ob_r.at[slot], of_hi(q))

    def xy_copy(k, q, slot):
        return remote(hs.at[q], rs.at[slot], rs_s.at[k], rs_r.at[slot], of_xy(q))

    def z_copy(k, q, slot):
        return remote(zb.at[zz], zb.at[slot], zb_s.at[k], zb_r.at[slot], of_z(q))

    def all_copy(k, q, slot):
        return remote(
            sum_ref.at[core, xy], sum_ref.at[core, slot], ag_s.at[k], ag_r.at[slot], of_xy(q)
        )

    def start(number, mine, copy):
        others(number, mine, lambda k, q: copy(k, q, mine).start())

    def arrive(number, mine, copy):
        others(number, mine, lambda k, q: copy(k, q, q).wait_recv())

    def sent(number, mine, copy):
        others(number, mine, lambda k, q: copy(k, q, mine).wait_send())

    start(4, zhi, pick_copy)

    fetches[1].wait()
    nbr = nbr_ref[...]
    device = (nbr * 43691) >> 19
    slot = nbr - 12 * device
    place = (((device >> 5) - slab + 1) * 3 + ((device & 31) - cross + 1)) * HOME + slot
    place = jnp.clip(place, 0, 9 * HOME - 1)
    lookup_vec[...] = jnp.where(nbr < 0, 9 * HOME, place)
    to_scalar = pltpu.make_async_copy(lookup_vec, lookup_ref, in_s.at[0])
    to_scalar.start()

    fetches[2].wait()
    build_first(w1_ref, w1p, t)
    fetches[3].wait()
    fetches[4].wait()
    for ref, i in ((bd2, 0), (bd3, 1)):
        ref[...] = jnp.zeros_like(ref)
        ref[0:128, 0:128] = wmid_ref[i]
        ref[128:256, 128:256] = wmid_ref[i]
    wl = wlast_ref[...].astype(F32)
    sub = lax.broadcasted_iota(jnp.int32, (128, 128), 0)
    for z in range(8):
        wle[:, 128 * z : 128 * z + 128] = jnp.where((sub & 7) == z, wl, 0.0).astype(BF16)
    fetches[5].wait()
    fetches[6].wait()
    source = target_ref[...].astype(F32)
    spread([source[:, 128 * i : 128 * i + 128] for i in range(4)], keep_in(tt), 8, 0)
    tab[9 * HOME] = jnp.zeros((8, 128), F32)

    def unpack(slot):
        packed[slot] = table[slot].astype(F32)
        parts = [packed[slot, HOME * i : HOME * i + HOME, :] for i in range(4)]

        def keep(y, tile):
            tab[HOME * slot : HOME * slot + HOME, y, :] = tile

        spread(parts, keep, 12, 2)

    def await_halo(k):
        @pl.when(near[k][0])
        def _():
            halo_copy(k, slot_of(*STEPS[k]), k).wait_recv()

    unpack(4)
    for group in (range(6, 8), range(6)):
        for k in group:
            await_halo(k)
        for k in group:
            unpack(slot_of(*STEPS[k]))

    to_scalar.wait()

    for b in range(HOME):
        build_window(b, lookup_ref, tab, pad, xs)

    live = jnp.full((8, 128), live_ref[0], jnp.int32)

    window = xs[...]
    predicted = jnp.zeros((ROWS, 128), F32)
    for j in range(4):
        col = slice(256 * j, 256 * j + 256)
        a = jnp.tanh(dot(window, t[:, col])).astype(BF16)
        h1[:, col] = a
        a = jnp.tanh(dot(a, bd2[...])).astype(BF16)
        h2[:, col] = a
        a = jnp.tanh(dot(a, bd3[...])).astype(BF16)
        h3[:, col] = a
        predicted += dot_n(a, wle[:, col])
    for b in range(HOME):
        tile = jnp.zeros((8, 128), F32)
        for k in range(8):
            part = predicted[64 * b + 8 * k : 64 * b + 8 * k + 8]
            tile = jnp.where(((lane >> 3) & 7) == k, part, tile)
        pt[8 * b : 8 * b + 8, :] = tile
    for i in range(3):
        at = 8 * (KEEP + 2 * i)
        extra[i] = jnp.where(lane < 64, pt[at : at + 8, :], pt[at + 8 : at + 16, :])
    eb[xc] = extra[...]
    start(8, xc, row_copy)
    for b in range(HOME):
        rows = slice(8 * b, 8 * b + 8)
        mask = jnp.where(b < live, 1.0, 0.0).astype(F32)
        res = ((pt[rows, :] * mask - tt[rows, :]) * mask / SCALE).astype(BF16).astype(F32)
        for k in range(4):
            both = jnp.concatenate(
                [
                    jnp.where((lane >> 3) == 2 * k, res, 0.0),
                    jnp.where((lane >> 3) == 2 * k + 1, res, 0.0),
                ],
                axis=0,
            )
            r2[64 * b + 16 * k : 64 * b + 16 * k + 16, :] = both.astype(BF16)
    rr = r2[...]
    for j in range(4):
        col = slice(256 * j, 256 * j + 256)
        h = h3[:, col].astype(F32)
        d = (dot(rr, wle[:, col]) * (1.0 - h * h)).astype(BF16)
        d3[:, col] = d
        h = h2[:, col].astype(F32)
        d = (dot_n(d, bd3[...]) * (1.0 - h * h)).astype(BF16)
        d2[:, col] = d
        h = h1[:, col].astype(F32)
        d = (dot_n(d, bd2[...]) * (1.0 - h * h)).astype(BF16)
        d1[:, col] = d

    second = jnp.zeros((128, 128), F32)
    third = jnp.zeros((128, 128), F32)
    for z in range(8):
        col = slice(128 * z, 128 * z + 128)
        second += dot_t(h1[:, col], d2[:, col])
        third += dot_t(h2[:, col], d3[:, col])
    flat[0:128, :] = second
    flat[128:256, :] = third

    total = jnp.zeros((WIN, 128), F32)
    xv = xs[...]
    for j in range(4):
        g = dot_t(xv, d1[:, 256 * j : 256 * j + 256])
        for i in range(2):
            z = 2 * j + i
            part = g[:, 128 * i : 128 * i + 128]
            total += part if z == 0 else pltpu.roll(part, WIN - z, 0)
    sums[...] = total
    for ax in range(5):
        for ay in range(5):
            at = 64 * ay + 12 * ax
            to = 256 + 25 * ax + 5 * ay
            flat[to : to + 5, :] = sums[at : at + 5, :]
    last = jnp.zeros((1, 128), F32)
    for j in range(4):
        g = dot_t(r2[...], h3[:, 256 * j : 256 * j + 256])
        for i in range(2):
            z = 2 * j + i
            part = jnp.where((sub & 7) == z, g[:, 128 * i : 128 * i + 128], 0.0)
            last += jnp.sum(part, axis=0, keepdims=True)
    flat[381:382, :] = last
    flat[382:384, :] = jnp.zeros((2, 128), F32)

    def half_of(c):
        return flat.at[pl.ds(pl.multiple_of(192 * c, 192), 192)]

    first_pair = remote(half_of(1 - core), cs, cs_s.at[0], cs_r.at[0], pair)
    first_pair.start()
    first_pair.wait_recv()
    half[...] = half_of(core)[...] + cs[...]
    for i in range(16):
        hs[i] = half[PIECE * i : PIECE * i + PIECE, :]
    start(16, xy, xy_copy)
    rs[xy] = hs[xy]

    arrive(4, zhi, pick_copy)
    arrive(8, xc, row_copy)
    ob[...] = jnp.zeros_like(ob)
    wants = [pk[q] for q in range(4)]

    @pl.loop(0, 8)
    def _(d):
        for i in range(3):
            tile = eb[d, i]
            swapped = shift(tile, 64)
            name = (zhi * 8 + d) * KEEP + 2 * i
            first = jnp.where(lane < 64, tile, swapped)
            other = jnp.where(lane < 64, swapped, tile)
            for q in range(4):
                old = ob[q]
                old = jnp.where(wants[q] == name, first, old)
                ob[q] = jnp.where(wants[q] == name + 1, other, old)

    start(4, zhi, out_copy)
    rb[zhi] = ob[zhi]

    arrive(16, xy, xy_copy)
    total = rs[0]
    for i in range(1, 16):
        total += rs[i]
    zb[zz] = total
    start(16, zz, z_copy)

    for b in range(KEEP):
        mask = jnp.where(b < live, 1.0, 0.0).astype(F32)
        pred_ref[8 * b : 8 * b + 8, :] = pt[8 * b : 8 * b + 8, :] * mask
    arrive(4, zhi, out_copy)
    tile = (rb[0] + rb[1]) + (rb[2] + rb[3])
    pred_ref[48:56, :] = tile
    pred_ref[56:64, :] = shift(tile, 64)

    for k in range(8):

        @pl.when(near[k][0])
        def _():
            halo_copy(k, 0, k).wait_send()

    sent(4, zhi, pick_copy)
    sent(8, xc, row_copy)
    sent(4, zhi, out_copy)
    first_pair.wait_send()
    sent(16, xy, xy_copy)

    arrive(16, zz, z_copy)
    total = zb[0]
    for i in range(1, 16):
        total += zb[i]
    sum_ref[core, xy] = total
    start(16, xy, all_copy)
    arrive(16, xy, all_copy)
    last_pair = remote(sum_ref.at[core], sum_ref.at[core], cs_s.at[1], cs_r.at[1], pair)
    last_pair.start()
    sent(16, zz, z_copy)
    sent(16, xy, all_copy)
    last_pair.wait_send()
    remote(
        sum_ref.at[1 - core], sum_ref.at[1 - core], cs_s.at[1], cs_r.at[1], pair
    ).wait_recv()


def write_kernel(sum_ref, tile_ref, pred_ref, gfirst_ref, gmid_ref, glast_ref, flat):
    for c in range(2):
        for i in range(16):
            at = 192 * c + PIECE * i
            flat[at : at + PIECE, :] = sum_ref[c, i]
    gmid_ref[0] = flat[0:128, :]
    gmid_ref[1] = flat[128:256, :]
    gfirst_ref[...] = flat[256:381, :]
    glast_ref[...] = flat[381:382, :]
    lane = lanes((8, 128))
    parts = [jnp.zeros((8, 128), F32) for _ in range(4)]
    for y in range(8):
        v = tile_ref[pl.ds(y, 8, stride=8), :]
        for x in range(8):
            low = 64 * (x % 2) + 8 * y
            inside = (lane >= low) & (lane < low + 8)
            parts[x // 2] = jnp.where(inside, shift(v, low - 8 * x), parts[x // 2])
    for i in range(4):
        pred_ref[:, 128 * i : 128 * i + 128] = parts[i]


def dma(n):
    return pltpu.SemaphoreType.DMA((n,))


def train(vof, target, neighbours, live_blocks, pick, w_first, w_mid, w_last):
    big = pltpu.VMEM((ROWS, 1024), BF16)
    piece = pltpu.VMEM((16, PIECE, 128), F32)
    tiles = pltpu.VMEM((4, 8, 128), F32)
    return pl.pallas_call(
        train_kernel,
        out_shape=(
            jax.ShapeDtypeStruct((2, 16, PIECE, 128), F32),
            jax.ShapeDtypeStruct((64, 128), F32),
        ),
        in_specs=[pl.BlockSpec(memory_space=pltpu.HBM)] * 8,
        out_specs=(VMEM, VMEM),
        scratch_shapes=[
            pltpu.VMEM((HOME, 512), BF16),
            pltpu.VMEM((HOME, 512), BF16),
            pltpu.VMEM((HOME, 26), jnp.int32),
            pltpu.SMEM((1,), jnp.int32),
            pltpu.VMEM((1, 2), jnp.int32),
            pltpu.VMEM((125, 128), BF16),
            pltpu.VMEM((2, 128, 128), BF16),
            pltpu.VMEM((1, 128), BF16),
            pltpu.VMEM((HOME, 26), jnp.int32),
            pltpu.SMEM((HOME, 26), jnp.int32),
            pltpu.VMEM((9, 48, 128), F32),
            pltpu.VMEM((9, 48, 128), BF16),
            pltpu.VMEM((9 * HOME + 1, 8, 128), F32),
            pltpu.VMEM((96, 128), F32),
            pltpu.VMEM((2 * HOME, 24, 128), F32),
            pltpu.VMEM((ROWS, WIN), BF16),
            pltpu.VMEM((128, 128), F32),
            pltpu.VMEM((WIN, 1024), BF16),
            pltpu.VMEM((256, 256), BF16),
            pltpu.VMEM((256, 256), BF16),
            pltpu.VMEM((128, 1024), BF16),
            big,
            big,
            big,
            big,
            big,
            big,
            pltpu.VMEM((ROWS, 128), BF16),
            pltpu.VMEM((96, 128), F32),
            pltpu.VMEM((384, 128), F32),
            pltpu.VMEM((384, 128), F32),
            pltpu.VMEM((3, 8, 128), F32),
            pltpu.VMEM((8, 3, 8, 128), F32),
            pltpu.VMEM((4, 8, 128), jnp.int32),
            tiles,
            tiles,
            pltpu.VMEM((192, 128), F32),
            pltpu.VMEM((192, 128), F32),
            piece,
            piece,
            piece,
            dma(8),
            dma(8),
            dma(8),
            dma(8),
            dma(8),
            dma(4),
            dma(4),
            dma(4),
            dma(4),
            dma(2),
            dma(2),
            dma(16),
            dma(16),
            dma(16),
            dma(16),
            dma(16),
            dma(16),
        ],
        compiler_params=pltpu.CompilerParams(
            collective_id=0, has_side_effects=True, vmem_limit_bytes=63 << 20
        ),
        name="train",
    )(vof, target, neighbours, live_blocks, pick, w_first, w_mid, w_last)


def shards(vof, target, neighbours, live_blocks, pick, w_first, w_mid, w_last):
    sums, tiles = train(
        vof,
        target,
        neighbours,
        live_blocks,
        pick,
        w_first,
        w_mid,
        w_last.reshape(1, 128),
    )
    pred, gfirst, gmid, glast = pl.pallas_call(
        write_kernel,
        out_shape=(
            jax.ShapeDtypeStruct((8, 512), F32),
            jax.ShapeDtypeStruct((125, 128), F32),
            jax.ShapeDtypeStruct((2, 128, 128), F32),
            jax.ShapeDtypeStruct((1, 128), F32),
        ),
        in_specs=[VMEM, VMEM],
        out_specs=(VMEM, VMEM, VMEM, VMEM),
        scratch_shapes=[pltpu.VMEM((384, 128), F32)],
        name="write",
    )(sums, tiles)
    return pred, gfirst, gmid, glast.reshape(128)


def solution(mesh):
    both = ("stream", "cross")
    return jax.shard_map(
        shards,
        mesh=mesh,
        in_specs=(
            P(both, None),
            P(both, None),
            P(both, None),
            P(both),
            P(both, None),
            P(),
            P(),
            P(),
        ),
        out_specs=(P(both, None), P(), P(), P()),
        check_vma=False,
    )
```

```python
import jax
import jax.numpy as jnp
from jax import lax
from jax.experimental import pallas as pl
from jax.experimental.pallas import tpu as pltpu
from jax.sharding import PartitionSpec as P

MESH = pl.DeviceIdType.MESH
F32 = jnp.float32
BF16 = jnp.bfloat16

KEEP = 6
HOME = 12
ROWS = 768
WIN = 384
SCALE = 1572864.0
SLABS = 16
CROSS = 32
PIECE = 12
VMEM = pl.BlockSpec(memory_space=pltpu.VMEM)


def lanes(shape):
    return lax.broadcasted_iota(jnp.int32, shape, len(shape) - 1)


def shift(x, by):
    by = by % 128
    return x if by == 0 else pltpu.roll(x, by, x.ndim - 1)


def spread(parts, store, stride, first):
    lane = lanes(parts[0].shape)
    for y in range(8):
        total = jnp.zeros_like(parts[0])
        for x in range(8):
            moved = shift(parts[x // 2], stride * x + first - (64 * (x % 2) + 8 * y))
            low = stride * x + first
            total = jnp.where((lane >= low) & (lane < low + 8), moved, total)
        store(y, total)


def keep_in(ref):
    def store(y, tile):
        ref[pl.ds(y, HOME, stride=8), :] = tile

    return store


def remote(src, dst, send, recv, device):
    return pltpu.make_async_remote_copy(
        src_ref=src,
        dst_ref=dst,
        send_sem=send,
        recv_sem=recv,
        device_id=device,
        device_id_type=MESH,
    )


def dot_t(a, b):
    return lax.dot_general(a, b, (((0,), (0,)), ((), ())), preferred_element_type=F32)


def dot_n(a, b):
    return lax.dot_general(a, b, (((1,), (1,)), ((), ())), preferred_element_type=F32)


def dot(a, b):
    return jnp.dot(a, b, preferred_element_type=F32)


def build_first(w1_ref, w1p, t):
    w1p[...] = jnp.zeros_like(w1p)
    w1p[0:125, :] = w1_ref[...].astype(F32)
    w1 = w1p[...].astype(BF16)
    k = lax.broadcasted_iota(jnp.int32, (WIN, 128), 0)
    f = lanes((WIN, 128))
    m = k & 63
    ax = (m * 43) >> 9
    zp = m - 12 * ax
    ay = k >> 6
    code = jnp.where((m < 60) & (ay < 5), 25 * ax + 5 * ay + zp, -1000)
    for z in range(8):
        hit = (f == code - z) & (zp >= z) & (zp < z + 5)
        select = jnp.where(hit, 1.0, 0.0).astype(BF16)
        t[:, 128 * z : 128 * z + 128] = dot(select, w1).astype(BF16)


def build_window(b, lookup_ref, tab, pad, xs):
    lane = lanes((8, 128))
    zp = lane - 12 * ((lane * 43) >> 9)
    for dy in range(3):
        row = []
        for dx in range(3):
            got = []
            for dz in range(3):
                k = 9 * dx + 3 * dy + dz
                if k == 13:
                    at = 4 * HOME + b
                else:
                    at = lookup_ref[b, k if k < 13 else k - 1]
                got.append(tab[at])
            row.append(
                jnp.where(zp < 2, shift(got[0], -8), jnp.where(zp < 10, got[1], shift(got[2], 8)))
            )
        low = jnp.where(lane < 24, shift(row[0], -72), shift(row[1], 24))
        high = jnp.where(lane < 72, shift(row[1], -24), shift(row[2], 72))
        pad[2 * b, 8 * dy : 8 * dy + 8, :] = low
        pad[2 * b + 1, 8 * dy : 8 * dy + 8, :] = high
    for half in range(2):
        a = [pad[2 * b + half, 6 + ay : 14 + ay, :] for ay in range(5)]
        odd = [shift(a[1], 64), shift(a[3], 64)]
        made = []
        for x in range(4):
            inside = (lane >= 12 * x) & (lane < 12 * x + 64)
            made.append(
                [
                    shift(jnp.where(inside, a[0], odd[0]), -12 * x),
                    shift(jnp.where(inside, a[2], odd[1]), -12 * x),
                    shift(a[4], -12 * x),
                ]
            )
        for pair in range(2):
            for g in range(3):
                both = jnp.concatenate([made[2 * pair][g], made[2 * pair + 1][g]], axis=0)
                base = 64 * b + 32 * half + 16 * pair
                xs[base : base + 16, 128 * g : 128 * g + 128] = both.astype(BF16)


STEPS = [(a, b) for a in (-1, 0, 1) for b in (-1, 0, 1) if (a, b) != (0, 0)]
STEPS.sort(key=lambda step: (step[1] == 0, step[0] == 0))


def train_kernel(
    vof_hbm,
    target_hbm,
    nbr_hbm,
    live_hbm,
    pick_hbm,
    w1_hbm,
    wmid_hbm,
    wlast_hbm,
    sum_ref,
    pred_ref,
    vof_ref,
    target_ref,
    nbr_ref,
    live_ref,
    pick_ref,
    w1_ref,
    wmid_ref,
    wlast_ref,
    lookup_vec,
    lookup_ref,
    packed,
    table,
    tab,
    tt,
    pad,
    xs,
    w1p,
    t,
    bd2,
    bd3,
    wle,
    h1,
    h2,
    h3,
    d1,
    d2,
    d3,
    r2,
    pt,
    flat,
    sums,
    extra,
    eb,
    pk,
    ob,
    rb,
    cs,
    half,
    hs,
    rs,
    zb,
    in_s,
    halo_s,
    halo_r,
    eb_s,
    eb_r,
    pk_s,
    pk_r,
    ob_s,
    ob_r,
    cs_s,
    cs_r,
    rs_s,
    rs_r,
    zb_s,
    zb_r,
    ag_s,
    ag_r,
):
    fetches = [
        pltpu.make_async_copy(src, dst, in_s.at[i])
        for i, (src, dst) in enumerate(
            (
                (vof_hbm, vof_ref),
                (nbr_hbm, nbr_ref),
                (w1_hbm, w1_ref),
                (wmid_hbm, wmid_ref),
                (wlast_hbm, wlast_ref),
                (target_hbm, target_ref),
                (live_hbm, live_ref),
                (pick_hbm, pick_ref),
            )
        )
    ]
    for fetch in fetches:
        fetch.start()

    slab = lax.axis_index("stream")
    cross = lax.axis_index("cross")
    zlo, y = slab // 4, lax.rem(slab, 4)
    zhi, xc = cross // 8, lax.rem(cross, 8)
    x, core = xc // 2, lax.rem(xc, 2)
    zz = zhi * 4 + zlo
    xy = y * 4 + x
    pair = (slab, cross + 1 - 2 * core)

    def of_xy(q):
        return (zlo * 4 + q // 4, zhi * 8 + 2 * lax.rem(q, 4) + core)

    def of_z(q):
        return (lax.rem(q, 4) * 4 + y, (q // 4) * 8 + xc)

    def of_hi(q):
        return (slab, q * 8 + xc)

    def of_row(q):
        return (slab, zhi * 8 + q)

    def others(number, mine, body):
        def step(k, carry):
            body(k, lax.rem(mine + k, number))
            return carry

        lax.fori_loop(1, number, step, 0)

    table[...] = jnp.zeros_like(table)

    barrier = pltpu.get_barrier_semaphore()

    def greet(device):
        pl.semaphore_signal(barrier, inc=1, device_id=device, device_id_type=MESH)

    others(16, zz, lambda k, q: greet(of_z(q)))
    near = []
    count = jnp.int32(15 + 15 + 7 + 1)
    for a, b in STEPS:
        valid = (slab + a >= 0) & (slab + a < SLABS) & (cross + b >= 0) & (cross + b < CROSS)
        device = (lax.rem(slab + a + SLABS, SLABS), lax.rem(cross + b + CROSS, CROSS))
        near.append((valid, device))
        count += jnp.where(valid, 1, 0)

        @pl.when(valid)
        def _():
            greet(device)

    others(16, xy, lambda k, q: greet(of_xy(q)))
    others(8, xc, lambda k, q: greet(of_row(q)))
    greet(pair)

    fetches[0].wait()
    rows = vof_ref[...].astype(F32)
    for i in range(4):
        packed[4, HOME * i : HOME * i + HOME, :] = rows[:, 128 * i : 128 * i + 128]
    table[4] = packed[4].astype(BF16)

    pl.semaphore_wait(barrier, count)

    def halo_copy(k, slot, sem):
        return remote(table.at[4], table.at[slot], halo_s.at[k], halo_r.at[sem], near[k][1])

    def slot_of(a, b):
        return (1 + a) * 3 + 1 + b

    for k, (a, b) in enumerate(STEPS):

        @pl.when(near[k][0])
        def _():
            halo_copy(k, slot_of(-a, -b), STEPS.index((-a, -b))).start()

    fetches[7].wait()
    lane = lanes((8, 128))
    pick = pick_ref[...]
    pk[zhi] = jnp.where(
        lane < 64,
        jnp.broadcast_to(pick[:, 0:1], (8, 128)),
        jnp.broadcast_to(pick[:, 1:2], (8, 128)),
    )

    def row_copy(k, q, slot):
        return remote(extra, eb.at[slot], eb_s.at[k], eb_r.at[slot], of_row(q))

    def pick_copy(k, q, slot):
        return remote(pk.at[zhi], pk.at[slot], pk_s.at[k], pk_r.at[slot], of_hi(q))

    def out_copy(k, q, slot):
        return remote(ob.at[q], rb.at[slot], ob_s.at[k], ob_r.at[slot], of_hi(q))

    def xy_copy(k, q, slot):
        return remote(hs.at[q], rs.at[slot], rs_s.at[k], rs_r.at[slot], of_xy(q))

    def z_copy(k, q, slot):
        return remote(zb.at[zz], zb.at[slot], zb_s.at[k], zb_r.at[slot], of_z(q))

    def all_copy(k, q, slot):
        return remote(
            sum_ref.at[core, xy], sum_ref.at[core, slot], ag_s.at[k], ag_r.at[slot], of_xy(q)
        )

    def start(number, mine, copy):
        others(number, mine, lambda k, q: copy(k, q, mine).start())

    def arrive(number, mine, copy):
        others(number, mine, lambda k, q: copy(k, q, q).wait_recv())

    def sent(number, mine, copy):
        others(number, mine, lambda k, q: copy(k, q, mine).wait_send())

    start(4, zhi, pick_copy)

    fetches[1].wait()
    nbr = nbr_ref[...]
    device = (nbr * 43691) >> 19
    slot = nbr - 12 * device
    place = (((device >> 5) - slab + 1) * 3 + ((device & 31) - cross + 1)) * HOME + slot
    place = jnp.clip(place, 0, 9 * HOME - 1)
    lookup_vec[...] = jnp.where(nbr < 0, 9 * HOME, place)
    to_scalar = pltpu.make_async_copy(lookup_vec, lookup_ref, in_s.at[0])
    to_scalar.start()

    fetches[2].wait()
    build_first(w1_ref, w1p, t)
    fetches[3].wait()
    fetches[4].wait()
    for ref, i in ((bd2, 0), (bd3, 1)):
        ref[...] = jnp.zeros_like(ref)
        ref[0:128, 0:128] = wmid_ref[i]
        ref[128:256, 128:256] = wmid_ref[i]
    wl = wlast_ref[...].astype(F32)
    sub = lax.broadcasted_iota(jnp.int32, (128, 128), 0)
    for z in range(8):
        wle[:, 128 * z : 128 * z + 128] = jnp.where((sub & 7) == z, wl, 0.0).astype(BF16)
    fetches[5].wait()
    fetches[6].wait()
    source = target_ref[...].astype(F32)
    spread([source[:, 128 * i : 128 * i + 128] for i in range(4)], keep_in(tt), 8, 0)
    tab[9 * HOME] = jnp.zeros((8, 128), F32)

    def unpack(slot):
        packed[slot] = table[slot].astype(F32)
        parts = [packed[slot, HOME * i : HOME * i + HOME, :] for i in range(4)]

        def keep(y, tile):
            tab[HOME * slot : HOME * slot + HOME, y, :] = tile

        spread(parts, keep, 12, 2)

    def await_halo(k):
        @pl.when(near[k][0])
        def _():
            halo_copy(k, slot_of(*STEPS[k]), k).wait_recv()

    unpack(4)
    for group in (range(6, 8), range(6)):
        for k in group:
            await_halo(k)
        for k in group:
            unpack(slot_of(*STEPS[k]))

    to_scalar.wait()

    for b in range(HOME):
        build_window(b, lookup_ref, tab, pad, xs)

    live = jnp.full((8, 128), live_ref[0], jnp.int32)

    window = xs[...]
    predicted = jnp.zeros((ROWS, 128), F32)
    for j in range(4):
        col = slice(256 * j, 256 * j + 256)
        a = jnp.tanh(dot(window, t[:, col])).astype(BF16)
        h1[:, col] = a
        a = jnp.tanh(dot(a, bd2[...])).astype(BF16)
        h2[:, col] = a
        a = jnp.tanh(dot(a, bd3[...])).astype(BF16)
        h3[:, col] = a
        predicted += dot_n(a, wle[:, col])
    for b in range(HOME):
        tile = jnp.zeros((8, 128), F32)
        for k in range(8):
            part = predicted[64 * b + 8 * k : 64 * b + 8 * k + 8]
            tile = jnp.where(((lane >> 3) & 7) == k, part, tile)
        pt[8 * b : 8 * b + 8, :] = tile
    for i in range(3):
        at = 8 * (KEEP + 2 * i)
        extra[i] = jnp.where(lane < 64, pt[at : at + 8, :], pt[at + 8 : at + 16, :])
    eb[xc] = extra[...]
    start(8, xc, row_copy)
    for b in range(HOME):
        rows = slice(8 * b, 8 * b + 8)
        mask = jnp.where(b < live, 1.0, 0.0).astype(F32)
        res = ((pt[rows, :] * mask - tt[rows, :]) * mask / SCALE).astype(BF16).astype(F32)
        for k in range(4):
            both = jnp.concatenate(
                [
                    jnp.where((lane >> 3) == 2 * k, res, 0.0),
                    jnp.where((lane >> 3) == 2 * k + 1, res, 0.0),
                ],
                axis=0,
            )
            r2[64 * b + 16 * k : 64 * b + 16 * k + 16, :] = both.astype(BF16)
    rr = r2[...]
    for j in range(4):
        col = slice(256 * j, 256 * j + 256)
        h = h3[:, col].astype(F32)
        d = (dot(rr, wle[:, col]) * (1.0 - h * h)).astype(BF16)
        d3[:, col] = d
        h = h2[:, col].astype(F32)
        d = (dot_n(d, bd3[...]) * (1.0 - h * h)).astype(BF16)
        d2[:, col] = d
        h = h1[:, col].astype(F32)
        d = (dot_n(d, bd2[...]) * (1.0 - h * h)).astype(BF16)
        d1[:, col] = d

    second = jnp.zeros((256, 256), F32)
    third = jnp.zeros((256, 256), F32)
    for j in range(4):
        col = slice(256 * j, 256 * j + 256)
        second += dot_t(h1[:, col], d2[:, col])
        third += dot_t(h2[:, col], d3[:, col])
    second = second[0:128, 0:128] + second[128:256, 128:256]
    third = third[0:128, 0:128] + third[128:256, 128:256]
    flat[0:128, :] = second
    flat[128:256, :] = third

    total = jnp.zeros((WIN, 128), F32)
    xv = xs[...]
    for j in range(4):
        g = dot_t(xv, d1[:, 256 * j : 256 * j + 256])
        for i in range(2):
            z = 2 * j + i
            part = g[:, 128 * i : 128 * i + 128]
            total += part if z == 0 else pltpu.roll(part, WIN - z, 0)
    sums[...] = total
    for ax in range(5):
        for ay in range(5):
            at = 64 * ay + 12 * ax
            to = 256 + 25 * ax + 5 * ay
            flat[to : to + 5, :] = sums[at : at + 5, :]
    last = jnp.zeros((1, 128), F32)
    for j in range(4):
        g = dot_t(r2[...], h3[:, 256 * j : 256 * j + 256])
        for i in range(2):
            z = 2 * j + i
            part = jnp.where((sub & 7) == z, g[:, 128 * i : 128 * i + 128], 0.0)
            last += jnp.sum(part, axis=0, keepdims=True)
    flat[381:382, :] = last
    flat[382:384, :] = jnp.zeros((2, 128), F32)

    def half_of(c):
        return flat.at[pl.ds(pl.multiple_of(192 * c, 192), 192)]

    first_pair = remote(half_of(1 - core), cs, cs_s.at[0], cs_r.at[0], pair)
    first_pair.start()
    first_pair.wait_recv()
    half[...] = half_of(core)[...] + cs[...]
    for i in range(16):
        hs[i] = half[PIECE * i : PIECE * i + PIECE, :]
    start(16, xy, xy_copy)
    rs[xy] = hs[xy]

    arrive(4, zhi, pick_copy)
    arrive(8, xc, row_copy)
    ob[...] = jnp.zeros_like(ob)
    wants = [pk[q] for q in range(4)]

    @pl.loop(0, 8)
    def _(d):
        for i in range(3):
            tile = eb[d, i]
            swapped = shift(tile, 64)
            name = (zhi * 8 + d) * KEEP + 2 * i
            first = jnp.where(lane < 64, tile, swapped)
            other = jnp.where(lane < 64, swapped, tile)
            for q in range(4):
                old = ob[q]
                old = jnp.where(wants[q] == name, first, old)
                ob[q] = jnp.where(wants[q] == name + 1, other, old)

    start(4, zhi, out_copy)
    rb[zhi] = ob[zhi]

    arrive(16, xy, xy_copy)
    total = rs[0]
    for i in range(1, 16):
        total += rs[i]
    zb[zz] = total
    start(16, zz, z_copy)

    for b in range(KEEP):
        mask = jnp.where(b < live, 1.0, 0.0).astype(F32)
        pred_ref[8 * b : 8 * b + 8, :] = pt[8 * b : 8 * b + 8, :] * mask
    arrive(4, zhi, out_copy)
    tile = (rb[0] + rb[1]) + (rb[2] + rb[3])
    pred_ref[48:56, :] = tile
    pred_ref[56:64, :] = shift(tile, 64)

    for k in range(8):

        @pl.when(near[k][0])
        def _():
            halo_copy(k, 0, k).wait_send()

    sent(4, zhi, pick_copy)
    sent(8, xc, row_copy)
    sent(4, zhi, out_copy)
    first_pair.wait_send()
    sent(16, xy, xy_copy)

    arrive(16, zz, z_copy)
    total = zb[0]
    for i in range(1, 16):
        total += zb[i]
    sum_ref[core, xy] = total
    start(16, xy, all_copy)
    arrive(16, xy, all_copy)
    last_pair = remote(sum_ref.at[core], sum_ref.at[core], cs_s.at[1], cs_r.at[1], pair)
    last_pair.start()
    sent(16, zz, z_copy)
    sent(16, xy, all_copy)
    last_pair.wait_send()
    remote(
        sum_ref.at[1 - core], sum_ref.at[1 - core], cs_s.at[1], cs_r.at[1], pair
    ).wait_recv()


def write_kernel(sum_ref, tile_ref, pred_ref, gfirst_ref, gmid_ref, glast_ref, flat):
    for c in range(2):
        for i in range(16):
            at = 192 * c + PIECE * i
            flat[at : at + PIECE, :] = sum_ref[c, i]
    gmid_ref[0] = flat[0:128, :]
    gmid_ref[1] = flat[128:256, :]
    gfirst_ref[...] = flat[256:381, :]
    glast_ref[...] = flat[381:382, :]
    lane = lanes((8, 128))
    parts = [jnp.zeros((8, 128), F32) for _ in range(4)]
    for y in range(8):
        v = tile_ref[pl.ds(y, 8, stride=8), :]
        for x in range(8):
            low = 64 * (x % 2) + 8 * y
            inside = (lane >= low) & (lane < low + 8)
            parts[x // 2] = jnp.where(inside, shift(v, low - 8 * x), parts[x // 2])
    for i in range(4):
        pred_ref[:, 128 * i : 128 * i + 128] = parts[i]


def dma(n):
    return pltpu.SemaphoreType.DMA((n,))


def train(vof, target, neighbours, live_blocks, pick, w_first, w_mid, w_last):
    big = pltpu.VMEM((ROWS, 1024), BF16)
    piece = pltpu.VMEM((16, PIECE, 128), F32)
    tiles = pltpu.VMEM((4, 8, 128), F32)
    return pl.pallas_call(
        train_kernel,
        out_shape=(
            jax.ShapeDtypeStruct((2, 16, PIECE, 128), F32),
            jax.ShapeDtypeStruct((64, 128), F32),
        ),
        in_specs=[pl.BlockSpec(memory_space=pltpu.HBM)] * 8,
        out_specs=(VMEM, VMEM),
        scratch_shapes=[
            pltpu.VMEM((HOME, 512), BF16),
            pltpu.VMEM((HOME, 512), BF16),
            pltpu.VMEM((HOME, 26), jnp.int32),
            pltpu.SMEM((1,), jnp.int32),
            pltpu.VMEM((1, 2), jnp.int32),
            pltpu.VMEM((125, 128), BF16),
            pltpu.VMEM((2, 128, 128), BF16),
            pltpu.VMEM((1, 128), BF16),
            pltpu.VMEM((HOME, 26), jnp.int32),
            pltpu.SMEM((HOME, 26), jnp.int32),
            pltpu.VMEM((9, 48, 128), F32),
            pltpu.VMEM((9, 48, 128), BF16),
            pltpu.VMEM((9 * HOME + 1, 8, 128), F32),
            pltpu.VMEM((96, 128), F32),
            pltpu.VMEM((2 * HOME, 24, 128), F32),
            pltpu.VMEM((ROWS, WIN), BF16),
            pltpu.VMEM((128, 128), F32),
            pltpu.VMEM((WIN, 1024), BF16),
            pltpu.VMEM((256, 256), BF16),
            pltpu.VMEM((256, 256), BF16),
            pltpu.VMEM((128, 1024), BF16),
            big,
            big,
            big,
            big,
            big,
            big,
            pltpu.VMEM((ROWS, 128), BF16),
            pltpu.VMEM((96, 128), F32),
            pltpu.VMEM((384, 128), F32),
            pltpu.VMEM((384, 128), F32),
            pltpu.VMEM((3, 8, 128), F32),
            pltpu.VMEM((8, 3, 8, 128), F32),
            pltpu.VMEM((4, 8, 128), jnp.int32),
            tiles,
            tiles,
            pltpu.VMEM((192, 128), F32),
            pltpu.VMEM((192, 128), F32),
            piece,
            piece,
            piece,
            dma(8),
            dma(8),
            dma(8),
            dma(8),
            dma(8),
            dma(4),
            dma(4),
            dma(4),
            dma(4),
            dma(2),
            dma(2),
            dma(16),
            dma(16),
            dma(16),
            dma(16),
            dma(16),
            dma(16),
        ],
        compiler_params=pltpu.CompilerParams(
            collective_id=0, has_side_effects=True, vmem_limit_bytes=63 << 20
        ),
        name="train",
    )(vof, target, neighbours, live_blocks, pick, w_first, w_mid, w_last)


def shards(vof, target, neighbours, live_blocks, pick, w_first, w_mid, w_last):
    sums, tiles = train(
        vof,
        target,
        neighbours,
        live_blocks,
        pick,
        w_first,
        w_mid,
        w_last.reshape(1, 128),
    )
    pred, gfirst, gmid, glast = pl.pallas_call(
        write_kernel,
        out_shape=(
            jax.ShapeDtypeStruct((8, 512), F32),
            jax.ShapeDtypeStruct((125, 128), F32),
            jax.ShapeDtypeStruct((2, 128, 128), F32),
            jax.ShapeDtypeStruct((1, 128), F32),
        ),
        in_specs=[VMEM, VMEM],
        out_specs=(VMEM, VMEM, VMEM, VMEM),
        scratch_shapes=[pltpu.VMEM((384, 128), F32)],
        name="write",
    )(sums, tiles)
    return pred, gfirst, gmid, glast.reshape(128)


def solution(mesh):
    both = ("stream", "cross")
    return jax.shard_map(
        shards,
        mesh=mesh,
        in_specs=(
            P(both, None),
            P(both, None),
            P(both, None),
            P(both),
            P(both, None),
            P(),
            P(),
            P(),
        ),
        out_specs=(P(both, None), P(), P(), P()),
        check_vma=False,
    )
```
